128 devices in a mesh: seq: 16 (over y, z_hi, core), head: 8 (over z_lo, x).
Axes of the slice: x: 4, y: 4, z: 4 (z_hi: 2, z_lo: 2; z = z_hi * 2 + z_lo), core: 2. Of those that a mesh axis runs over, the one named last changes fastest.
Arguments:
- query: bfloat16 [8192, 5120], P('seq', 'head'), may hold values from -6 to 6
- key_rows: bfloat16 [8192, 5120], P('seq', 'head'), may hold values from -6 to 6
- value_rows: bfloat16 [8192, 5120], P('seq', 'head'), may hold values from -6 to 6
- frame_seq: int32 [8192], replicated, may hold values from 0 to 3, never falling along the last dimension, each value on 1 to 3072 neighbouring positions
- order: int32 [32], replicated, may hold values from 0 to 31, each once
- w_out: bfloat16 [5120, 5120], P('head'), may hold values from -0.078125 to 0.078125
Outputs:
- mixed: bfloat16 [8192, 5120], P('seq', 'head')
The draws below stay inside these ranges and needn't reach their ends.
Inputs may be any that keep to these rules, and one draw needn't show every extreme that they name: `frame_seq`: frames never fall along the sequence; each of the 4 frames holds 1 to 3072 tokens, and one holds exactly 3072. `order`: a permutation: every block number appears once.
All inputs are finite; a program needn't handle non-finite values.
Results may differ from the reference program's by a relative error of at most 0.019.
Values may be sent and summed in bfloat16 or wider, within the bound.
No kernel may reach another device: no remote copies, remote signals or barrier semaphores. Data moves between devices by JAX's collectives and lax.ppermute only.
A program may use at most 256 MiB of HBM per device.

```python
import math
import jax
import jax.numpy as jnp
import numpy as np
from jax import lax

D = 5120
HEADS = 40
HEAD_DIM = 128
FRAMES = 4
TOKENS = 8192
GROUPS = 32
MOST_FRAME = 3072


def draw_query(key, part):
    key = jax.random.fold_in(key, 1)
    values = jnp.clip(jax.random.normal(key, (TOKENS, HEADS * HEAD_DIM)), -6.0, 6.0)
    return values.astype(jnp.bfloat16)


def draw_key_rows(key, part):
    key = jax.random.fold_in(key, 2)
    values = jnp.clip(jax.random.normal(key, (TOKENS, HEADS * HEAD_DIM)), -6.0, 6.0)
    return values.astype(jnp.bfloat16)


def steps_of(rng, dims, cuts, low, largest):
    loudness = 1.0
    for dim, blocks in cuts:
        steps = jax.random.uniform(jax.random.fold_in(jax.random.fold_in(rng, 6), dim), (blocks,), jnp.float32, low / len(cuts), largest / len(cuts))
        loudness = loudness * jnp.repeat(jnp.exp(steps), dims[dim] // blocks).reshape((-1,) + (1,) * (len(dims) - 1 - dim))
    return loudness


def split_up(number_of, total, bound, lean):
    loads = [(1 << 20) // math.isqrt(standing ** lean) + 1 for standing in range(2, number_of + 1)]
    spare, counts = total - bound - (number_of - 1), [1] * (number_of - 1)
    while spare > 0:
        movable = [i for i in range(number_of - 1) if counts[i] < bound]
        pool, budget = sum([loads[i] for i in movable]), spare
        for i in movable:
            extra = min(bound - counts[i], max(1, budget * loads[i] // pool), spare)
            counts[i] = counts[i] + extra
            spare = spare - extra
    return np.array([bound] + counts)


def ragged_sizes(stream_key, amount, total, reach, lean):
    if amount == 2:
        one = jax.random.randint(stream_key, (), max(1, total - reach), min(reach, total - 1) + 1)
        return jnp.stack([one, total - one])
    tallies = jnp.asarray(split_up(amount, total, reach, lean), jnp.int32)
    twos = (amount - 1) // 2
    donor, receiver = tallies[1:1 + 2 * twos:2], tallies[2:2 + 2 * twos:2]
    slack = jnp.minimum(donor - 1, reach - receiver)
    passed = jax.random.randint(jax.random.fold_in(stream_key, 1), (twos,), 0, 1 << 20) % (slack + 1)
    tallies = tallies.at[1:1 + 2 * twos:2].set(donor - passed).at[2:2 + 2 * twos:2].set(receiver + passed)
    return tallies[jax.random.permutation(jax.random.fold_in(stream_key, 2), amount)]


def noise(key, dims, spread, most, split=(), dtype=jnp.bfloat16):
    loudness = steps_of(key, dims, split, -0.22, 0.18) if split else 1.0
    entries = jax.random.normal(key, dims, jnp.float32) * spread * loudness
    return jnp.minimum(jnp.maximum(entries, -most), most).astype(dtype)


def setup_inputs(seed: int = 0) -> dict:
    keys = jax.random.split(jax.random.key(seed), 7)
    return {
        "query": draw_query(jax.random.fold_in(keys[6], 71), 0),
        "key_rows": draw_key_rows(jax.random.fold_in(keys[6], 71), 0),
        "value_rows": noise(keys[2], (TOKENS, HEADS * HEAD_DIM), 1.0, 6.0, ((0, 16), (1, 8))),
        "frame_seq": jnp.searchsorted(jnp.cumsum(ragged_sizes(keys[3], FRAMES, TOKENS, MOST_FRAME, 0)), jnp.arange(TOKENS), side="right").astype(jnp.int32),
        "order": jax.random.permutation(keys[4], GROUPS).astype(jnp.int32),
        "w_out": noise(keys[5], (HEADS * HEAD_DIM, D), (HEADS * HEAD_DIM) ** -0.5, 0.078125, ((0, 8),)),
    }


def reference(query, key_rows, value_rows, frame_seq, order, w_out):
    group_len = TOKENS // GROUPS
    frames = frame_seq.reshape(GROUPS, group_len)[order].reshape(TOKENS)
    scale = HEAD_DIM ** -0.5
    block = math.gcd(TOKENS, 1024)
    q_heads = query.reshape(TOKENS, HEADS, HEAD_DIM).transpose(1, 0, 2)
    k_heads = key_rows.reshape(TOKENS, HEADS, HEAD_DIM).transpose(1, 0, 2)
    v_heads = value_rows.reshape(TOKENS, HEADS, HEAD_DIM).transpose(1, 0, 2)

    def one_head(operands):
        q_one, k_one, v_one = operands

        def one_block(start):
            q_block = lax.dynamic_slice_in_dim(q_one, start, block, 0)
            f_block = lax.dynamic_slice_in_dim(frames, start, block, 0)
            scores = jnp.dot(q_block, k_one.T, preferred_element_type=jnp.float32) * scale
            allowed = frames[None, :] <= f_block[:, None]
            top = jnp.max(jnp.where(allowed, scores, -1e30), axis=1, keepdims=True)
            expo = jnp.where(allowed, jnp.exp(scores - top), 0.0)
            numer = jnp.dot(expo.astype(jnp.bfloat16), v_one, preferred_element_type=jnp.float32)
            return numer / jnp.sum(expo, axis=1, keepdims=True)

        starts = (jnp.arange(TOKENS // block) * block).astype(jnp.int32)
        return lax.map(one_block, starts).reshape(TOKENS, HEAD_DIM)

    attended = lax.map(one_head, (q_heads, k_heads, v_heads))
    attended = attended.transpose(1, 0, 2).reshape(TOKENS, HEADS * HEAD_DIM).astype(jnp.bfloat16)
    return jnp.dot(attended, w_out, preferred_element_type=jnp.float32).astype(jnp.bfloat16)
```

```python
import functools
import math

import jax
import jax.numpy as jnp
from jax import lax
from jax.experimental import pallas as pl
from jax.experimental.pallas import tpu as pltpu
from jax.sharding import PartitionSpec as P

HEAD_DIM = 128
BLOCK = 256
FRAMES = 4
BIG = 1e30
SCALE = HEAD_DIM ** (-0.5) * math.log2(math.e)
KEYS_STEP = 512
MIB = 1024 * 1024


def linear(y, zh, core, zl, x):
    return (((y % 4) * 2 + zh) * 2 + core) * 8 + zl * 4 + x % 4


def moved(move):
    pairs = []
    for y in range(4):
        for zh in range(2):
            for core in range(2):
                for zl in range(2):
                    for x in range(4):
                        at = (y, zh, core, zl, x)
                        pairs.append((linear(*at), linear(*move(*at))))
    return pairs


CORE = moved(lambda y, zh, core, zl, x: (y, zh, 1 - core, zl, x))
Z_HI = moved(lambda y, zh, core, zl, x: (y, 1 - zh, core, zl, x))


def y_shift(step):
    return moved(lambda y, zh, core, zl, x: (y + step, zh, core, zl, x))


def send(value, pairs):
    return lax.ppermute(value, ("seq", "head"), pairs)


def three_pieces(value):
    high = value.astype(jnp.bfloat16)
    rest = value - high.astype(jnp.float32)
    middle = rest.astype(jnp.bfloat16)
    low = (rest - middle.astype(jnp.float32)).astype(jnp.bfloat16)
    return high, middle, low


def attention_kernel(
    first, heads, blocks_total, order_ref, frames_ref, *refs
):
    q_parts, kv_parts = refs[:4], refs[4:8]
    keep_ref, give_ref = refs[8:10]
    q_all, k_all, v_all, mask_all, top_ref, acc_ref, base_ref, kv_sem, q_sem = refs[10:]
    width = heads * HEAD_DIM
    seq_at = lax.axis_index("seq")
    y_at = lax.shift_right_logical(seq_at, 2)
    column_at = lax.rem(seq_at, 4)
    tokens = blocks_total * BLOCK

    ends = []
    for f in range(FRAMES - 1):
        below = jnp.where(frames_ref[...] <= f, 1.0, 0.0)
        ends.append(jnp.sum(below).astype(jnp.int32))
    ends.append(jnp.int32(tokens))

    bases = []
    for part in range(4):
        row = lax.rem(y_at + part, 4)
        for half in range(2):
            bases.append(order_ref[row * 8 + column_at * 2 + half] * BLOCK)
    copies = []
    for i in range(8):
        rank = jnp.int32(0)
        for j in range(8):
            if j != i:
                rank = rank + jnp.where(bases[j] < bases[i], 1, 0)
        base_ref[rank] = bases[i]
        rows = pl.ds((i % 2) * BLOCK, BLOCK)
        to = pl.ds(pl.multiple_of(rank * BLOCK, BLOCK), BLOCK)
        part = kv_parts[i // 2]
        for n, (dst, at) in enumerate(((k_all, 0), (v_all, width))):
            copy = pltpu.make_async_copy(
                part.at[rows, pl.ds(at, width)], dst.at[to, :], kv_sem.at[2 * i + n]
            )
            copy.start()
            copies.append(copy)
    for part in range(4):
        copy = pltpu.make_async_copy(
            q_parts[part].at[:, pl.ds(first * HEAD_DIM, width)],
            q_all.at[pl.ds(part * 512, 512), :],
            q_sem.at[part],
        )
        copy.start()
        copies.append(copy)

    lane = lax.broadcasted_iota(jnp.int32, (BLOCK, HEAD_DIM), 1)
    offset = lax.broadcasted_iota(jnp.int32, (BLOCK, HEAD_DIM), 0)
    lane_end = jnp.where(
        lane == 0, ends[0], jnp.where(lane == 1, ends[1], jnp.where(lane == 2, ends[2], tokens))
    )
    lane_start = jnp.where(
        lane == 0, 0, jnp.where(lane == 1, ends[0], jnp.where(lane == 2, ends[1], ends[2]))
    )
    for slot in range(8):
        token = base_ref[slot] + offset
        hidden = (token >= lane_end) & (lane < FRAMES)
        mask_all[pl.ds(slot * BLOCK, BLOCK), :] = jnp.where(hidden, -BIG, 0.0).astype(jnp.bfloat16)
    for copy in copies:
        copy.wait()

    ones = jnp.ones((KEYS_STEP, HEAD_DIM), jnp.bfloat16)

    def one_block(index, out_ref, out_at, order_at):
        base = order_ref[order_at] * BLOCK
        last = base + (BLOCK - 1)
        limit = jnp.where(
            last < ends[0], ends[0],
            jnp.where(last < ends[1], ends[1], jnp.where(last < ends[2], ends[2], tokens)),
        )
        count = jnp.int32(0)
        for slot in range(8):
            count = count + jnp.where(base_ref[slot] < limit, 1, 0)
        steps = jnp.maximum(lax.div(count * BLOCK + (KEYS_STEP - 1), KEYS_STEP), 1)
        token = base + offset
        own = (token >= lane_start) & (token < lane_end) & (lane < FRAMES)
        own_frame = jnp.where(own, 1.0, 0.0).astype(jnp.bfloat16)
        top_ref[...] = jnp.full(top_ref.shape, -2.0 * BIG, jnp.float32)
        acc_ref[...] = jnp.zeros(acc_ref.shape, jnp.float32)
        q_rows = pl.ds(pl.multiple_of(index * BLOCK, BLOCK), BLOCK)

        def step(at, carry):
            rows = pl.ds(pl.multiple_of(at * KEYS_STEP, KEYS_STEP), KEYS_STEP)
            hidden = mask_all[rows, :]
            for h in range(heads):
                cols = pl.ds(h * HEAD_DIM, HEAD_DIM)
                q_ext = jnp.concatenate([q_all[q_rows, cols], own_frame], axis=1)
                k_ext = jnp.concatenate([k_all[rows, cols], hidden], axis=1)
                scores = lax.dot_general(
                    q_ext, k_ext, (((1,), (1,)), ((), ())), preferred_element_type=jnp.float32
                )
                before = top_ref[h]
                top = jnp.maximum(before[:, :1], jnp.max(scores, axis=1, keepdims=True))
                expo = jnp.exp2((scores - top) * SCALE).astype(jnp.bfloat16)
                shrink = jnp.exp2((before[:, :1] - top) * SCALE)
                v_ext = jnp.concatenate([v_all[rows, cols], ones], axis=1)
                added = jnp.dot(expo, v_ext, preferred_element_type=jnp.float32)
                acc_ref[h] = acc_ref[h] * shrink + added
                top_ref[h] = jnp.broadcast_to(top, (BLOCK, HEAD_DIM))
            return carry

        lax.fori_loop(0, steps, step, 0)
        out_rows = pl.ds(pl.multiple_of(out_at * BLOCK, BLOCK), BLOCK)
        stats = jnp.zeros((BLOCK, HEAD_DIM), jnp.bfloat16)
        for h in range(heads):
            total = acc_ref[h, :, HEAD_DIM:]
            out_ref[out_rows, pl.ds(h * HEAD_DIM, HEAD_DIM)] = (
                acc_ref[h, :, :HEAD_DIM] / total
            ).astype(jnp.bfloat16)
            log_sum = top_ref[h] * SCALE + jnp.log2(total)
            for n, piece in enumerate(three_pieces(log_sum)):
                stats = jnp.where(lane == 3 * h + n, piece, stats)
        out_ref[out_rows, pl.ds(width, HEAD_DIM)] = stats

    def blocks(n, carry):
        part = lax.div(n, 2)
        half = lax.rem(n, 2)
        flip_core = lax.rem(part, 2)
        flip_z = lax.div(part, 2)
        core = lax.rem(column_at, 2)
        zh = lax.div(column_at, 2)
        core_at = core + flip_core - 2 * core * flip_core
        z_at = zh + flip_z - 2 * zh * flip_z
        order_at = y_at * 8 + z_at * 4 + core_at * 2 + half
        out_at = flip_z * 2 + half

        @pl.when(flip_core == 0)
        def _():
            one_block(n, keep_ref, out_at, order_at)

        @pl.when(flip_core == 1)
        def _():
            one_block(n, give_ref, out_at, order_at)

        return carry

    lax.fori_loop(0, 8, blocks, 0)


def attention(first, heads, order, frames, q_parts, kv_parts):
    width = heads * HEAD_DIM
    part_shape = jax.ShapeDtypeStruct((1024, width + HEAD_DIM), jnp.bfloat16)
    any_spec = pl.BlockSpec(memory_space=pl.ANY)
    vmem_spec = pl.BlockSpec(memory_space=pltpu.VMEM)
    return pl.pallas_call(
        functools.partial(attention_kernel, first, heads, order.shape[0]),
        out_shape=(part_shape, part_shape),
        in_specs=[pl.BlockSpec(memory_space=pltpu.SMEM), vmem_spec] + [any_spec] * 8,
        out_specs=(vmem_spec, vmem_spec),
        scratch_shapes=[
            pltpu.VMEM((2048, width), jnp.bfloat16),
            pltpu.VMEM((2048, width), jnp.bfloat16),
            pltpu.VMEM((2048, width), jnp.bfloat16),
            pltpu.VMEM((2048, HEAD_DIM), jnp.bfloat16),
            pltpu.VMEM((heads, BLOCK, HEAD_DIM), jnp.float32),
            pltpu.VMEM((heads, BLOCK, 2 * HEAD_DIM), jnp.float32),
            pltpu.SMEM((8,), jnp.int32),
            pltpu.SemaphoreType.DMA((16,)),
            pltpu.SemaphoreType.DMA((4,)),
        ],
        compiler_params=pltpu.CompilerParams(vmem_limit_bytes=40 * MIB),
        cost_estimate=pl.CostEstimate(
            flops=heads * 2048 * 2048 * 128 * 8, bytes_accessed=8 * MIB, transcendentals=0
        ),
    )(order, frames, *q_parts, *kv_parts)


def merged(heads, mine, theirs):
    lane_at = heads * HEAD_DIM
    values, sums = [], []
    for h in range(heads):
        logs = []
        for ref in (mine, theirs):
            pieces = [
                ref[:, pl.ds(lane_at + 3 * h + n, 1)].astype(jnp.float32) for n in range(3)
            ]
            logs.append(pieces[0] + pieces[1] + pieces[2])
        top = jnp.maximum(logs[0], logs[1])
        first, second = jnp.exp2(logs[0] - top), jnp.exp2(logs[1] - top)
        total = first + second
        cols = pl.ds(h * HEAD_DIM, HEAD_DIM)
        values.append(
            mine[:, cols].astype(jnp.float32) * (first / total)
            + theirs[:, cols].astype(jnp.float32) * (second / total)
        )
        sums.append(top + jnp.log2(total))
    return values, sums


def merge_kernel(heads, with_sums, mine, theirs, out):
    values, sums = merged(heads, mine, theirs)
    for h in range(heads):
        out[:, pl.ds(h * HEAD_DIM, HEAD_DIM)] = values[h].astype(jnp.bfloat16)
    if with_sums:
        rows = out.shape[0]
        lane = lax.broadcasted_iota(jnp.int32, (rows, HEAD_DIM), 1)
        stats = jnp.zeros((rows, HEAD_DIM), jnp.bfloat16)
        for h in range(heads):
            for n, piece in enumerate(three_pieces(sums[h])):
                stats = jnp.where(lane == 3 * h + n, piece, stats)
        out[:, pl.ds(heads * HEAD_DIM, HEAD_DIM)] = stats


def merge(heads, mine, theirs, with_sums):
    rows = mine.shape[0]
    width = heads * HEAD_DIM + (HEAD_DIM if with_sums else 0)
    tile = 256
    spec = pl.BlockSpec((tile, heads * HEAD_DIM + HEAD_DIM), lambda i: (i, 0))
    return pl.pallas_call(
        functools.partial(merge_kernel, heads, with_sums),
        out_shape=jax.ShapeDtypeStruct((rows, width), jnp.bfloat16),
        grid=(rows // tile,),
        in_specs=[spec, spec],
        out_specs=pl.BlockSpec((tile, width), lambda i: (i, 0)),
        compiler_params=pltpu.CompilerParams(vmem_limit_bytes=16 * MIB),
        cost_estimate=pl.CostEstimate(
            flops=rows * width * 8, bytes_accessed=rows * width * 6, transcendentals=0
        ),
    )(mine, theirs)


CHUNKS = ((0, 5),)


def on_device(query, key_rows, value_rows, frame_seq, order, w_out):
    frames = frame_seq.reshape(64, 128)
    q_core = send(query, CORE)
    q_z = send(query, Z_HI)
    q_both = send(q_z, CORE)
    q_parts = (query, q_core, q_z, q_both)
    attended = []
    for first, heads in CHUNKS:
        cols = slice(first * HEAD_DIM, (first + heads) * HEAD_DIM)
        kv = jnp.concatenate([key_rows[:, cols], value_rows[:, cols]], axis=1)
        kv_parts = (kv, send(kv, y_shift(-1)), send(kv, y_shift(2)), send(kv, y_shift(1)))
        keep, give = attention(first, heads, order, frames, q_parts, kv_parts)
        both = merge(heads, keep, send(give, CORE), True)
        got = send(both[512:], Z_HI)
        attended.append(merge(heads, both[:512], got, False))
    joined = jnp.concatenate(attended, axis=1)
    partial_sum = jnp.dot(joined, w_out, preferred_element_type=jnp.float32)
    return lax.psum_scatter(
        partial_sum.astype(jnp.bfloat16), "head", scatter_dimension=1, tiled=True
    )


def solution(mesh):
    return jax.shard_map(
        on_device,
        mesh=mesh,
        in_specs=(P("seq", "head"), P("seq", "head"), P("seq", "head"), P(), P(), P("head", None)),
        out_specs=P("seq", "head"),
        check_vma=False,
    )
```

```python
import functools
import math

import jax
import jax.numpy as jnp
from jax import lax
from jax.experimental import pallas as pl
from jax.experimental.pallas import tpu as pltpu
from jax.sharding import Mesh
from jax.sharding import PartitionSpec as P

HEAD_DIM = 128
BLOCK = 256
FRAMES = 4
BIG = 1e30
SCALE = HEAD_DIM ** (-0.5) * math.log2(math.e)
KEYS_STEP = 512
MIB = 1024 * 1024
CHUNKS = ((0, 3), (3, 2))
ANY = pl.BlockSpec(memory_space=pl.ANY)
SMEM = pl.BlockSpec(memory_space=pltpu.SMEM)
VMEM = pl.BlockSpec(memory_space=pltpu.VMEM)


def send(value, axis, step):
    size = {"y": 4, "x": 4}.get(axis, 2)
    return lax.ppermute(value, axis, [(i, (i + step) % size) for i in range(size)])


def after(value, *done):
    return lax.optimization_barrier((value, *done))[0]


def three_pieces(value):
    high = value.astype(jnp.bfloat16)
    rest = value - high.astype(jnp.float32)
    middle = rest.astype(jnp.bfloat16)
    low = (rest - middle.astype(jnp.float32)).astype(jnp.bfloat16)
    return high, middle, low


def tables_kernel(order_ref, frames_ref, meta_ref, k_mask_ref, q_frame_ref, base_ref):
    y_at, zh_at, core_at = (lax.axis_index(a) for a in ("y", "zh", "core"))
    tokens = order_ref.shape[0] * BLOCK
    ends = []
    for f in range(FRAMES - 1):
        below = jnp.where(frames_ref[...] <= f, 1.0, 0.0)
        ends.append(jnp.sum(below).astype(jnp.int32))
    bases = []
    for part in range(4):
        row = lax.rem(y_at + part, 4)
        for half in range(2):
            bases.append(order_ref[row * 8 + zh_at * 4 + core_at * 2 + half] * BLOCK)
    for i in range(8):
        rank = jnp.int32(0)
        for j in range(8):
            if j != i:
                rank = rank + jnp.where(bases[j] < bases[i], 1, 0)
        base_ref[rank] = bases[i]
        meta_ref[i] = rank
    lane = lax.broadcasted_iota(jnp.int32, (BLOCK, HEAD_DIM), 1)
    offset = lax.broadcasted_iota(jnp.int32, (BLOCK, HEAD_DIM), 0)
    lane_end = jnp.where(
        lane == 0, ends[0], jnp.where(lane == 1, ends[1], jnp.where(lane == 2, ends[2], tokens))
    )
    lane_start = jnp.where(
        lane == 0, 0, jnp.where(lane == 1, ends[0], jnp.where(lane == 2, ends[1], ends[2]))
    )
    for n in range(8):
        rows = pl.ds(n * BLOCK, BLOCK)
        token = base_ref[n] + offset
        hidden = (token >= lane_end) & (lane < FRAMES)
        k_mask_ref[rows, :] = jnp.where(hidden, -BIG, 0.0).astype(jnp.bfloat16)
        flip_core, flip_z, half = (n // 2) % 2, n // 4, n % 2
        c = 1 - core_at if flip_core else core_at
        z = 1 - zh_at if flip_z else zh_at
        base = order_ref[y_at * 8 + z * 4 + c * 2 + half] * BLOCK
        last = base + (BLOCK - 1)
        limit = jnp.where(
            last < ends[0], ends[0],
            jnp.where(last < ends[1], ends[1], jnp.where(last < ends[2], ends[2], tokens)),
        )
        count = jnp.int32(0)
        for slot in range(8):
            count = count + jnp.where(bases[slot] < limit, 1, 0)
        meta_ref[8 + n] = jnp.maximum(lax.div(count * BLOCK + (KEYS_STEP - 1), KEYS_STEP), 1)
        token = base + offset
        own = (token >= lane_start) & (token < lane_end) & (lane < FRAMES)
        q_frame_ref[rows, :] = jnp.where(own, 1.0, 0.0).astype(jnp.bfloat16)


def tables(order, frames):
    table = jax.ShapeDtypeStruct((2048, HEAD_DIM), jnp.bfloat16)
    return pl.pallas_call(
        tables_kernel,
        out_shape=(jax.ShapeDtypeStruct((16,), jnp.int32), table, table),
        in_specs=[SMEM, VMEM],
        out_specs=(SMEM, VMEM, VMEM),
        scratch_shapes=[pltpu.SMEM((8,), jnp.int32)],
        compiler_params=pltpu.CompilerParams(vmem_limit_bytes=8 * MIB),
        cost_estimate=pl.CostEstimate(flops=MIB, bytes_accessed=MIB, transcendentals=0),
    )(order, frames)


def attention_kernel(first, heads, meta_ref, *refs):
    k_mask, q_frame = refs[:2]
    q_parts, kv_parts = refs[2:6], refs[6:10]
    keep_ref, give_ref = refs[10:12]
    mask_all, frame_all, q_all, k_all, v_all, out_all, in_sem, out_sem = refs[12:]
    width = heads * HEAD_DIM
    copies = []

    def start(src, dst):
        copy = pltpu.make_async_copy(src, dst, in_sem.at[len(copies)])
        copy.start()
        copies.append(copy)

    for i in range(8):
        rows = pl.ds((i % 2) * BLOCK, BLOCK)
        to = pl.ds(pl.multiple_of(meta_ref[i] * BLOCK, BLOCK), BLOCK)
        part = kv_parts[i // 2]
        start(part.at[rows, pl.ds(0, width)], k_all.at[to, :])
        start(part.at[rows, pl.ds(width, width)], v_all.at[to, :])
    start(k_mask, mask_all)
    start(q_frame, frame_all)
    for part in range(4):
        start(
            q_parts[part].at[:, pl.ds(first * HEAD_DIM, width)],
            q_all.at[pl.ds(part * 512, 512), :],
        )
    lane = lax.broadcasted_iota(jnp.int32, (BLOCK, HEAD_DIM), 1)
    ones = jnp.ones((2048, HEAD_DIM), jnp.bfloat16)
    for copy in copies:
        copy.wait()

    def whole_prefix(length, rows):
        stats = jnp.zeros((BLOCK, HEAD_DIM), jnp.bfloat16)
        hidden = mask_all[:length, :]
        own_frame = frame_all[rows, :]
        for h in range(heads):
            cols = pl.ds(h * HEAD_DIM, HEAD_DIM)
            q_ext = jnp.concatenate([q_all[rows, cols], own_frame], axis=1)
            k_ext = jnp.concatenate([k_all[:length, cols], hidden], axis=1)
            scores = lax.dot_general(
                q_ext, k_ext, (((1,), (1,)), ((), ())), preferred_element_type=jnp.float32
            )
            top = jnp.max(scores, axis=1, keepdims=True)
            expo = jnp.exp2((scores - top) * SCALE).astype(jnp.bfloat16)
            v_ext = jnp.concatenate([v_all[:length, cols], ones[:length]], axis=1)
            acc = jnp.dot(expo, v_ext, preferred_element_type=jnp.float32)
            total = acc[:, HEAD_DIM:]
            out_all[rows, cols] = (acc[:, :HEAD_DIM] / total).astype(jnp.bfloat16)
            log_sum = top * SCALE + jnp.log2(total)
            for n, piece in enumerate(three_pieces(log_sum)):
                stats = jnp.where(lane == 3 * h + n, piece, stats)
        out_all[rows, pl.ds(width, HEAD_DIM)] = stats

    def out_copy(part, half, dst, at):
        return pltpu.make_async_copy(
            out_all.at[pl.ds(part * 512 + half * BLOCK, BLOCK), :],
            dst.at[pl.ds(at * 512 + half * BLOCK, BLOCK), :],
            out_sem.at[part * 2 + half],
        )

    parts = ((1, give_ref, 0), (3, give_ref, 1), (0, keep_ref, 0), (2, keep_ref, 1))
    for part, dst, at in parts:

        def one_block(half, carry, part=part):
            n = part * 2 + half
            rows = pl.ds(pl.multiple_of(n * BLOCK, BLOCK), BLOCK)
            steps = meta_ref[8 + n]
            for count in range(1, 2048 // KEYS_STEP + 1):

                @pl.when(steps == count)
                def _(count=count):
                    whole_prefix(count * KEYS_STEP, rows)

            return carry

        lax.fori_loop(0, 2, one_block, 0)
        for half in range(2):
            out_copy(part, half, dst, at).start()
    for part, dst, at in parts:
        for half in range(2):
            out_copy(part, half, dst, at).wait()


def attention(first, heads, meta, k_mask, q_frame, q_parts, kv_parts):
    width = heads * HEAD_DIM
    part_shape = jax.ShapeDtypeStruct((1024, width + HEAD_DIM), jnp.bfloat16)
    table = pltpu.VMEM((2048, HEAD_DIM), jnp.bfloat16)
    wide = pltpu.VMEM((2048, width), jnp.bfloat16)
    return pl.pallas_call(
        functools.partial(attention_kernel, first, heads),
        out_shape=(part_shape, part_shape),
        in_specs=[SMEM] + [ANY] * 10,
        out_specs=(ANY, ANY),
        scratch_shapes=[
            table,
            table,
            wide,
            wide,
            wide,
            pltpu.VMEM((2048, width + HEAD_DIM), jnp.bfloat16),
            pltpu.SemaphoreType.DMA((22,)),
            pltpu.SemaphoreType.DMA((8,)),
        ],
        compiler_params=pltpu.CompilerParams(vmem_limit_bytes=40 * MIB),
        cost_estimate=pl.CostEstimate(
            flops=heads * 2048 * 2048 * 128 * 8, bytes_accessed=8 * MIB, transcendentals=0
        ),
    )(meta, k_mask, q_frame, *q_parts, *kv_parts)


def merge_kernel(heads, with_sums, mine, theirs, out):
    rows = out.shape[0]
    lane_at = heads * HEAD_DIM
    lane = lax.broadcasted_iota(jnp.int32, (rows, HEAD_DIM), 1)
    stats = jnp.zeros((rows, HEAD_DIM), jnp.bfloat16)
    for h in range(heads):
        logs = []
        for ref in (mine, theirs):
            pieces = [
                ref[:, pl.ds(lane_at + 3 * h + n, 1)].astype(jnp.float32) for n in range(3)
            ]
            logs.append(pieces[0] + pieces[1] + pieces[2])
        top = jnp.maximum(logs[0], logs[1])
        first, second = jnp.exp2(logs[0] - top), jnp.exp2(logs[1] - top)
        total = first + second
        cols = pl.ds(h * HEAD_DIM, HEAD_DIM)
        out[:, cols] = (
            mine[:, cols].astype(jnp.float32) * (first / total)
            + theirs[:, cols].astype(jnp.float32) * (second / total)
        ).astype(jnp.bfloat16)
        if with_sums:
            for n, piece in enumerate(three_pieces(top + jnp.log2(total))):
                stats = jnp.where(lane == 3 * h + n, piece, stats)
    if with_sums:
        out[:, pl.ds(lane_at, HEAD_DIM)] = stats


def merge(heads, mine, theirs, with_sums, first_row=0, rows=512):
    width = heads * HEAD_DIM + (HEAD_DIM if with_sums else 0)
    tile = 256
    skip = first_row // tile
    there = skip if theirs.shape[0] > rows else 0
    full = heads * HEAD_DIM + HEAD_DIM
    return pl.pallas_call(
        functools.partial(merge_kernel, heads, with_sums),
        out_shape=jax.ShapeDtypeStruct((rows, width), jnp.bfloat16),
        grid=(rows // tile,),
        in_specs=[
            pl.BlockSpec((tile, full), lambda i: (i + skip, 0)),
            pl.BlockSpec((tile, full), lambda i: (i + there, 0)),
        ],
        out_specs=pl.BlockSpec((tile, width), lambda i: (i, 0)),
        compiler_params=pltpu.CompilerParams(vmem_limit_bytes=16 * MIB),
        cost_estimate=pl.CostEstimate(
            flops=rows * width * 8, bytes_accessed=rows * width * 6, transcendentals=0
        ),
    )(mine, theirs)


def project_kernel(chunks, give, mine_ref, other_ref, *refs):
    gathered = refs[: len(chunks)]
    rest = refs[len(chunks):]
    before = None
    if len(rest) == 5:
        before, out_ref, w_all, g_sem, w_sem = rest
    else:
        out_ref, w_all, g_sem, w_sem = rest
    x_at, core_at = lax.axis_index("x"), lax.axis_index("core")
    copies = []
    total_heads = sum(heads for _, heads in chunks)
    for part in range(4):
        at = lax.rem(x_at + part, 4)
        done = 0
        for first, heads in chunks:
            for h in range(heads):
                for ref, core in ((mine_ref, core_at), (other_ref, 1 - core_at)):
                    row = (at * total_heads + done) * HEAD_DIM + core * 64
                    copy = pltpu.make_async_copy(
                        ref.at[pl.ds(part * 320 + (first + h) * 64, 64), pl.ds(give * 640, 640)],
                        w_all.at[pl.ds(pl.multiple_of(row, 64), 64), :],
                        w_sem.at[len(copies)],
                    )
                    copy.start()
                    copies.append(copy)
                done += 1
    del g_sem
    for copy in copies:
        copy.wait()
    total = before[...] if before is not None else None
    for x in range(4):
        done = 0
        for (first, heads), ref in zip(chunks, gathered):
            row = (x * total_heads + done) * HEAD_DIM
            term = jnp.dot(
                ref[x], w_all[pl.ds(row, heads * HEAD_DIM), :],
                preferred_element_type=jnp.float32,
            )
            total = term if total is None else total + term
            done += heads
    out_ref[...] = total.astype(out_ref.dtype)


def project(chunks, give, mine, other, gathered, before, dtype):
    heads = sum(h for _, h in chunks)
    operands = [mine, other, *gathered] + ([before] if before is not None else [])
    return pl.pallas_call(
        functools.partial(project_kernel, chunks, give),
        out_shape=jax.ShapeDtypeStruct((512, 640), dtype),
        in_specs=[ANY, ANY] + [VMEM] * (len(operands) - 2),
        out_specs=VMEM,
        scratch_shapes=[
            pltpu.VMEM((4 * heads * HEAD_DIM, 640), jnp.bfloat16),
            pltpu.SemaphoreType.DMA((1,)),
            pltpu.SemaphoreType.DMA((8 * heads,)),
        ],
        compiler_params=pltpu.CompilerParams(vmem_limit_bytes=40 * MIB),
        cost_estimate=pl.CostEstimate(
            flops=2 * 512 * 640 * 512 * heads, bytes_accessed=6 * MIB, transcendentals=0
        ),
    )(*operands)


def weight_parts(w_out):
    core_at, zl_at, x_at = (lax.axis_index(a) for a in ("core", "zl", "x"))
    half = lax.dynamic_index_in_dim(w_out.reshape(5, 2, 64, 5120), core_at, 1, keepdims=False)
    half = half.reshape(320, 5120)
    parts = []
    for distance in range(4):
        x = (x_at + distance) % 4
        columns = [
            lax.dynamic_slice_in_dim(half, (z * 4 + x) * 640, 640, 1) for z in (zl_at, 1 - zl_at)
        ]
        parts.append(jnp.concatenate(columns, axis=1))
    return parts


def on_device(query, key_rows, value_rows, frame_seq, order, w_out):
    meta, k_mask, q_frame = tables(order, frame_seq.reshape(64, 128))
    kv_all = [
        jnp.concatenate(
            [a[:, first * HEAD_DIM : (first + heads) * HEAD_DIM] for a in (key_rows, value_rows)],
            axis=1,
        )
        for first, heads in CHUNKS
    ]
    q_z = send(query, "zh", 1)
    q_core = send(query, "core", 1)
    kv_parts = []
    for kv in kv_all:
        if kv_parts:
            kv = after(kv, *kv_parts[-1][1:])
        kv_parts.append((kv, send(kv, "y", -1), send(kv, "y", 2), send(kv, "y", 1)))
    q_both = send(q_z, "core", 1)
    q_parts = (query, q_core, q_z, q_both)

    w_parts = weight_parts(w_out)
    w_two = send(after(w_parts[2], q_core), "x", 2)
    w_one = send(after(w_parts[1], q_z), "x", 1)
    w_three = send(after(w_parts[3], w_two), "x", -1)
    w_mine = jnp.concatenate([w_parts[0], w_three, w_two, w_one], axis=0)
    w_other = send(w_mine, "core", 1)

    gathered = []
    for (first, heads), kv in zip(CHUNKS, kv_parts):
        keep, give = attention(first, heads, meta, k_mask, q_frame, q_parts, kv)
        theirs = send(give, "core", 1)
        out_z = merge(heads, keep, theirs, True, first_row=512)
        got = send(out_z, "zh", 1)
        own = merge(heads, keep, theirs, True, first_row=0)
        done = merge(heads, own, got, False)
        gathered.append(lax.all_gather(done, "x", axis=0))

    sent = None
    for n, chunk in enumerate(CHUNKS):
        last = n == len(CHUNKS) - 1
        sent = project(
            (chunk,), 1, w_mine, w_other, gathered[n : n + 1], sent,
            jnp.bfloat16 if last else jnp.float32,
        )
    came = send(sent, "zl", 1)
    kept = project(CHUNKS, 0, w_mine, w_other, gathered, None, jnp.float32)
    return (kept + came.astype(jnp.float32)).astype(jnp.bfloat16)


def solution(mesh):
    fine = Mesh(mesh.devices.reshape(4, 2, 2, 2, 4), ("y", "zh", "core", "zl", "x"))
    rows, columns = ("y", "zh", "core"), ("zl", "x")
    return jax.shard_map(
        on_device,
        mesh=fine,
        in_specs=(P(rows, columns),) * 3 + (P(), P(), P(columns, None)),
        out_specs=P(rows, columns),
        check_vma=False,
    )
```

```python
import functools
import math

import jax
import jax.numpy as jnp
from jax import lax
from jax.experimental import pallas as pl
from jax.experimental.pallas import tpu as pltpu
from jax.sharding import Mesh
from jax.sharding import PartitionSpec as P

HEAD_DIM = 128
HEADS = 5
WIDTH = HEADS * HEAD_DIM
BLOCK = 256
FRAMES = 4
BIG = 1e30
SCALE = HEAD_DIM ** (-0.5) * math.log2(math.e)
MIB = 1024 * 1024
STAGES = (((0, 0), (0, 1)), ((1, 0), (3, 0)), ((1, 1), (3, 1)), ((2, 0), (2, 1)))
SMEM = pl.BlockSpec(memory_space=pltpu.SMEM)
VMEM = pl.BlockSpec(memory_space=pltpu.VMEM)
SMALL = pl.CostEstimate(flops=1024, bytes_accessed=1024, transcendentals=0)


def send(value, axis, step):
    size = {"y": 4, "x": 4}.get(axis, 2)
    return lax.ppermute(value, axis, [(i, (i + step) % size) for i in range(size)])


def after(value, *done):
    return lax.optimization_barrier((value, *done))[0]


def three_pieces(value):
    high = value.astype(jnp.bfloat16).astype(jnp.float32)
    rest = value - high
    middle = rest.astype(jnp.bfloat16).astype(jnp.float32)
    low = rest - middle
    return (high + pltpu.roll(middle, 8, 1) + pltpu.roll(low, 16, 1)).astype(jnp.bfloat16)


def tables_kernel(order_ref, frames_ref, meta_ref, k_mask_ref, q_frame_ref, base_ref):
    y_at, zh_at, core_at = (lax.axis_index(a) for a in ("y", "zh", "core"))
    tokens = order_ref.shape[0] * BLOCK
    ends = []
    for f in range(FRAMES - 1):
        below = jnp.where(frames_ref[...] <= f, 1.0, 0.0)
        ends.append(jnp.sum(below).astype(jnp.int32))
    lane = lax.broadcasted_iota(jnp.int32, (BLOCK, HEAD_DIM), 1)
    offset = lax.broadcasted_iota(jnp.int32, (BLOCK, HEAD_DIM), 0)
    lane_end = jnp.where(
        lane == 0, ends[0], jnp.where(lane == 1, ends[1], jnp.where(lane == 2, ends[2], tokens))
    )
    lane_start = jnp.where(
        lane == 0, 0, jnp.where(lane == 1, ends[0], jnp.where(lane == 2, ends[1], ends[2]))
    )
    stage_bases = []
    for stage, parts in enumerate(STAGES):
        bases = []
        for dy, dc in parts:
            row = lax.rem(y_at + dy, 4)
            core = 1 - core_at if dc else core_at
            for half in range(2):
                bases.append(order_ref[row * 8 + zh_at * 4 + core * 2 + half] * BLOCK)
        for i, base in enumerate(bases):
            rank = jnp.int32(0)
            for j, other in enumerate(bases):
                if j != i:
                    rank = rank + jnp.where(other < base, 1, 0)
            base_ref[4 * stage + rank] = base
            meta_ref[4 * stage + i] = rank
        stage_bases.append(bases)
    for n in range(16):
        token = base_ref[n] + offset
        hidden = (token >= lane_end) & (lane < FRAMES)
        k_mask_ref[pl.ds(n * BLOCK, BLOCK), :] = jnp.where(hidden, -BIG, 0.0).astype(jnp.bfloat16)
    for n in range(4):
        z = 1 - zh_at if n < 2 else zh_at
        base = order_ref[y_at * 8 + z * 4 + core_at * 2 + n % 2] * BLOCK
        last = base + (BLOCK - 1)
        limit = jnp.where(
            last < ends[0], ends[0],
            jnp.where(last < ends[1], ends[1], jnp.where(last < ends[2], ends[2], tokens)),
        )
        for stage, bases in enumerate(stage_bases):
            count = jnp.int32(0)
            for base_k in bases:
                count = count + jnp.where(base_k < limit, 1, 0)
            meta_ref[16 + 4 * stage + n] = count
        token = base + offset
        own = (token >= lane_start) & (token < lane_end) & (lane < FRAMES)
        q_frame_ref[pl.ds(n * BLOCK, BLOCK), :] = jnp.where(own, 1.0, 0.0).astype(jnp.bfloat16)


def tables(order, frames):
    return pl.pallas_call(
        tables_kernel,
        out_shape=(
            jax.ShapeDtypeStruct((32,), jnp.int32),
            jax.ShapeDtypeStruct((4096, HEAD_DIM), jnp.bfloat16),
            jax.ShapeDtypeStruct((1024, HEAD_DIM), jnp.bfloat16),
        ),
        in_specs=[SMEM, VMEM],
        out_specs=(SMEM, VMEM, VMEM),
        scratch_shapes=[pltpu.SMEM((16,), jnp.int32)],
        compiler_params=pltpu.CompilerParams(vmem_limit_bytes=8 * MIB),
        cost_estimate=SMALL,
    )(order, frames)


def attention_kernel(stage, first, count_q, n_kv, meta_ref, k_mask, q_frame, *refs):
    q_parts, kv_parts = refs[:2], refs[2 : 2 + n_kv]
    rest = refs[2 + n_kv :]
    if stage:
        o_in, log_in = rest[:2]
        rest = rest[2:]
    last = stage == len(STAGES) - 1
    if last:
        out, k_all, v_all, q_all = rest
    else:
        out, log_out, k_all, v_all, q_all = rest
    per_part = 4 // n_kv
    for i in range(4):
        rows = pl.ds((i % per_part) * BLOCK, BLOCK)
        to = pl.ds(pl.multiple_of(meta_ref[4 * stage + i] * BLOCK, BLOCK), BLOCK)
        part = kv_parts[i // per_part]
        k_all[to, :] = part[rows, pl.ds(0, WIDTH)]
        v_all[to, :] = part[rows, pl.ds(WIDTH, WIDTH)]
    for n in range(count_q):
        half = pl.ds(((first + n) % 2) * BLOCK, BLOCK)
        q_all[pl.ds(n * BLOCK, BLOCK), :] = q_parts[(first + n) // 2][half, :]
    lane = lax.broadcasted_iota(jnp.int32, (BLOCK, HEAD_DIM), 1)
    ones = jnp.ones((4 * BLOCK, HEAD_DIM), jnp.bfloat16)

    def one_block(n, carry):
        at = first + n
        rows = pl.ds(pl.multiple_of(n * BLOCK, BLOCK), BLOCK)
        rows_at = pl.ds(pl.multiple_of(at * BLOCK, BLOCK), BLOCK)
        count = meta_ref[16 + 4 * stage + at]

        def put_logs(logs):
            if last:
                out[rows, pl.ds(WIDTH, HEAD_DIM)] = three_pieces(logs)
            else:
                log_out[rows, :] = logs

        def prefix(length):
            hidden = k_mask[pl.ds(4 * stage * BLOCK, length), :]
            own_frame = q_frame[rows_at, :]
            logs = jnp.zeros((BLOCK, HEAD_DIM), jnp.float32)
            for h in range(HEADS):
                cols = pl.ds(h * HEAD_DIM, HEAD_DIM)
                q_ext = jnp.concatenate([q_all[rows, cols], own_frame], axis=1)
                k_ext = jnp.concatenate([k_all[:length, cols], hidden], axis=1)
                scores = lax.dot_general(
                    q_ext, k_ext, (((1,), (1,)), ((), ())), preferred_element_type=jnp.float32
                )
                top = jnp.max(scores, axis=1, keepdims=True)
                expo = jnp.exp2((scores - top) * SCALE).astype(jnp.bfloat16)
                v_ext = jnp.concatenate([v_all[:length, cols], ones[:length]], axis=1)
                acc = jnp.dot(expo, v_ext, preferred_element_type=jnp.float32)
                value, total = acc[:, :HEAD_DIM], acc[:, HEAD_DIM:]
                top = jnp.broadcast_to(top * SCALE, (BLOCK, HEAD_DIM))
                if stage:
                    log = jnp.broadcast_to(log_in[rows_at, pl.ds(h, 1)], (BLOCK, HEAD_DIM))
                    both = jnp.maximum(log, top)
                    new, old = jnp.exp2(top - both), jnp.exp2(log - both)
                    value = value * new + o_in[rows_at, cols] * old
                    total = total * new + old
                    top = both
                out[rows, cols] = (value / total).astype(out.dtype)
                logs = jnp.where(lane == h, top + jnp.log2(total), logs)
            put_logs(logs)

        if stage:

            @pl.when(count == 0)
            def _():
                out[rows, pl.ds(0, WIDTH)] = o_in[rows_at, :].astype(out.dtype)
                put_logs(log_in[rows_at, :])

        steps = count if stage else jnp.maximum(count, 1)
        for length in range(1, 5):

            @pl.when(steps == length)
            def _(length=length):
                prefix(length * BLOCK)

        return carry

    lax.fori_loop(0, count_q, one_block, 0)


def attention(stage, blocks, meta, k_mask, q_frame, q_parts, kv_parts, state=()):
    first, count_q = blocks
    rows = count_q * BLOCK
    if stage == len(STAGES) - 1:
        out_shape = (jax.ShapeDtypeStruct((rows, WIDTH + HEAD_DIM), jnp.bfloat16),)
    else:
        out_shape = (
            jax.ShapeDtypeStruct((rows, WIDTH), jnp.float32),
            jax.ShapeDtypeStruct((rows, HEAD_DIM), jnp.float32),
        )
    return pl.pallas_call(
        functools.partial(attention_kernel, stage, first, count_q, len(kv_parts)),
        out_shape=out_shape,
        in_specs=[SMEM] + [VMEM] * (4 + len(kv_parts) + len(state)),
        out_specs=(VMEM,) * len(out_shape),
        scratch_shapes=[pltpu.VMEM((n, WIDTH), jnp.bfloat16) for n in (1024, 1024, rows)],
        compiler_params=pltpu.CompilerParams(vmem_limit_bytes=30 * MIB),
        cost_estimate=SMALL,
    )(meta, k_mask, q_frame, *q_parts, *kv_parts, *state)


def merge_kernel(mine, theirs, out):
    logs = []
    for ref in (mine, theirs):
        pieces = ref[:, pl.ds(WIDTH, HEAD_DIM)].astype(jnp.float32)
        logs.append(
            pieces + pltpu.roll(pieces, HEAD_DIM - 8, 1) + pltpu.roll(pieces, HEAD_DIM - 16, 1)
        )
    top = jnp.maximum(logs[0], logs[1])
    first, second = jnp.exp2(logs[0] - top), jnp.exp2(logs[1] - top)
    total = first + second
    first, second = first / total, second / total
    for h in range(HEADS):
        cols = pl.ds(h * HEAD_DIM, HEAD_DIM)
        out[:, cols] = (
            mine[:, cols].astype(jnp.float32) * first[:, h : h + 1]
            + theirs[:, cols].astype(jnp.float32) * second[:, h : h + 1]
        ).astype(jnp.bfloat16)


def merge(mine, theirs, block):
    full = WIDTH + HEAD_DIM
    return pl.pallas_call(
        merge_kernel,
        out_shape=jax.ShapeDtypeStruct((BLOCK, WIDTH), jnp.bfloat16),
        grid=(1,),
        in_specs=[
            pl.BlockSpec((BLOCK, full), lambda i: (block, 0)),
            pl.BlockSpec((BLOCK, full), lambda i: (0, 0)),
        ],
        out_specs=pl.BlockSpec((BLOCK, WIDTH), lambda i: (0, 0)),
        compiler_params=pltpu.CompilerParams(vmem_limit_bytes=8 * MIB),
        cost_estimate=SMALL,
    )(mine, theirs)


def join_kernel(k_ref, v_ref, out_ref, sem):
    copies = [
        pltpu.make_async_copy(ref, out_ref.at[:, pl.ds(n * WIDTH, WIDTH)], sem.at[n])
        for n, ref in enumerate((k_ref, v_ref))
    ]
    for copy in copies:
        copy.start()
    for copy in copies:
        copy.wait()


def join(keys, values):
    return pl.pallas_call(
        join_kernel,
        out_shape=jax.ShapeDtypeStruct((512, 2 * WIDTH), jnp.bfloat16),
        in_specs=[pl.BlockSpec(memory_space=pl.ANY)] * 2,
        out_specs=VMEM,
        scratch_shapes=[pltpu.SemaphoreType.DMA((2,))],
        compiler_params=pltpu.CompilerParams(vmem_limit_bytes=8 * MIB),
        cost_estimate=SMALL,
    )(keys, values)


def project_kernel(give, *refs):
    mine, other, parts, out_ref = refs[:4], refs[4:8], refs[8:13], refs[13]
    core_at, zl_at = lax.axis_index("core"), lax.axis_index("zl")

    def run(weights):
        rows = [
            parts[0][...],
            parts[1][...],
            jnp.concatenate([parts[2][...], parts[3][...]], axis=0),
            parts[4][...],
        ]
        total = None
        for row, w in zip(rows, weights):
            term = jnp.dot(row, w[...], preferred_element_type=jnp.float32)
            total = term if total is None else total + term
        out_ref[...] = total.astype(out_ref.dtype)

    same = core_at == zl_at

    @pl.when(same != give)
    def _():
        run(mine)

    @pl.when(same == give)
    def _():
        run(other)


def project(give, w_mine, w_other, parts, dtype):
    return pl.pallas_call(
        functools.partial(project_kernel, give),
        out_shape=jax.ShapeDtypeStruct((BLOCK, 640), dtype),
        in_specs=[VMEM] * 13,
        out_specs=VMEM,
        compiler_params=pltpu.CompilerParams(vmem_limit_bytes=12 * MIB),
        cost_estimate=SMALL,
    )(*w_mine, *w_other, *parts)


def together(*groups):
    flat, tree = jax.tree.flatten(groups)
    return jax.tree.unflatten(tree, lax.optimization_barrier(tuple(flat)))


def on_device(query, key_rows, value_rows, frame_seq, order, w_out):
    core_at, x_at = lax.axis_index("core"), lax.axis_index("x")

    def columns(zl, distance):
        return lax.dynamic_slice_in_dim(w_out, (zl * 4 + (x_at + distance) % 4) * 640, 640, 1)

    kv = join(key_rows, value_rows)
    kv_next = send(kv, "y", -1)
    kv_back = send(kv, "y", 1)
    q_z = send(query, "zh", 1)
    kv_core = send(kv, "core", 1)
    w_far = send(columns(core_at, 2), "x", 2)
    args = (*tables(order, frame_seq.reshape(64, 128)), (q_z, query))
    state = attention(0, (0, 4), *args, (kv, kv_core))
    kv_next, kv_back, w_far, state = together(kv_next, kv_back, w_far, state)

    far_low = send(kv_next[:BLOCK], "y", -1)
    far_high = send(kv_back[BLOCK:], "y", 1)
    next_core = send(kv_next, "core", 1)
    back_core = send(kv_back, "core", 1)
    w_next = send(after(columns(core_at, 3), w_far), "x", -1)
    state = attention(1, (0, 4), *args, (kv_next, kv_back), state)
    far_low, far_high, state = together(far_low, far_high, state)
    far = [far_low, far_high, send(far_low, "core", 1), send(far_high, "core", 1)]
    w_back = send(after(columns(core_at, 1), far_low), "x", 1)
    state = attention(2, (0, 4), *args, (next_core, back_core), state)
    far, w_next, state = together(far, w_next, state)

    got = []
    for block in range(2):
        (give,) = attention(3, (block, 1), *args, far, state)
        got.append(send(give, "zh", 1))
    (keep,) = attention(3, (2, 2), *args, far, state)
    w_mine = (columns(core_at, 0), w_next, w_far, w_back)
    w_other = [columns(1 - core_at, 0)] + [send(w, "core", 1) for w in w_mine[1:]]

    out = []
    for block, their in enumerate(got):
        done = merge(keep, their, block)
        one, three = send(done, "x", -1), send(done, "x", 1)
        low, high = send(one[:128], "x", -1), send(three[128:], "x", 1)
        out.append([done, one, low, high, three])

    came = [
        send(project(True, w_mine, w_other, parts, jnp.bfloat16), "zl", 1) for parts in out
    ]
    kept = [project(False, w_mine, w_other, parts, jnp.float32) for parts in out]
    return jnp.concatenate(
        [(a + b.astype(jnp.float32)).astype(jnp.bfloat16) for a, b in zip(kept, came)], axis=0
    )


def solution(mesh):
    fine = Mesh(mesh.devices.reshape(4, 2, 2, 2, 4), ("y", "zh", "core", "zl", "x"))
    rows, columns = ("y", "zh", "core"), ("zl", "x")
    return jax.shard_map(
        on_device,
        mesh=fine,
        in_specs=(P(rows, columns),) * 3 + (P(), P(), P(columns, None)),
        out_specs=P(rows, columns),
        check_vma=False,
    )
```

```python
import functools
import math

import jax
import jax.numpy as jnp
from jax import lax
from jax.experimental import pallas as pl
from jax.experimental.pallas import tpu as pltpu
from jax.sharding import Mesh
from jax.sharding import PartitionSpec as P

HEAD_DIM = 128
HEADS = 5
WIDTH = HEADS * HEAD_DIM
BLOCK = 256
FRAMES = 4
BIG = 1e30
SCALE = HEAD_DIM ** (-0.5) * math.log2(math.e)
MIB = 1024 * 1024
SLOT = {(0, 0): 0, (0, 1): 2, (1, 0): 4, (3, 0): 6, (1, 1): 8, (3, 1): 10, (2, 0): 12, (2, 1): 14}
SMEM = pl.BlockSpec(memory_space=pltpu.SMEM)
VMEM = pl.BlockSpec(memory_space=pltpu.VMEM)
SMALL = pl.CostEstimate(flops=1024, bytes_accessed=1024, transcendentals=0)


def send(value, axis, step):
    size = {"y": 4, "x": 4}.get(axis, 2)
    return lax.ppermute(value, axis, [(i, (i + step) % size) for i in range(size)])


def after(value, *done):
    return lax.optimization_barrier((value, *done))[0]


def three_pieces(value):
    high = value.astype(jnp.bfloat16).astype(jnp.float32)
    rest = value - high
    middle = rest.astype(jnp.bfloat16).astype(jnp.float32)
    low = rest - middle
    return (high + pltpu.roll(middle, 8, 1) + pltpu.roll(low, 16, 1)).astype(jnp.bfloat16)


def tables_kernel(order_ref, frames_ref, k_mask_ref, q_frame_ref):
    y_at, zh_at, core_at = (lax.axis_index(a) for a in ("y", "zh", "core"))
    tokens = order_ref.shape[0] * BLOCK
    ends = []
    for f in range(FRAMES - 1):
        below = jnp.where(frames_ref[...] <= f, 1.0, 0.0)
        ends.append(jnp.sum(below).astype(jnp.int32))
    lane = lax.broadcasted_iota(jnp.int32, (BLOCK, HEAD_DIM), 1)
    offset = lax.broadcasted_iota(jnp.int32, (BLOCK, HEAD_DIM), 0)
    lane_end = jnp.where(
        lane == 0, ends[0], jnp.where(lane == 1, ends[1], jnp.where(lane == 2, ends[2], tokens))
    )
    lane_start = jnp.where(
        lane == 0, 0, jnp.where(lane == 1, ends[0], jnp.where(lane == 2, ends[1], ends[2]))
    )
    for (dy, dc), slot in SLOT.items():
        row = lax.rem(y_at + dy, 4)
        core = 1 - core_at if dc else core_at
        for half in range(2):
            token = order_ref[row * 8 + zh_at * 4 + core * 2 + half] * BLOCK + offset
            hidden = (token >= lane_end) & (lane < FRAMES)
            k_mask_ref[pl.ds((slot + half) * BLOCK, BLOCK), :] = jnp.where(
                hidden, -BIG, 0.0
            ).astype(jnp.bfloat16)
    for n in range(4):
        z = 1 - zh_at if n < 2 else zh_at
        token = order_ref[y_at * 8 + z * 4 + core_at * 2 + n % 2] * BLOCK + offset
        own = (token >= lane_start) & (token < lane_end) & (lane < FRAMES)
        q_frame_ref[pl.ds(n * BLOCK, BLOCK), :] = jnp.where(own, 1.0, 0.0).astype(jnp.bfloat16)


def tables(order, frames):
    return pl.pallas_call(
        tables_kernel,
        out_shape=(
            jax.ShapeDtypeStruct((4096, HEAD_DIM), jnp.bfloat16),
            jax.ShapeDtypeStruct((1024, HEAD_DIM), jnp.bfloat16),
        ),
        in_specs=[SMEM, VMEM],
        out_specs=(VMEM, VMEM),
        compiler_params=pltpu.CompilerParams(vmem_limit_bytes=8 * MIB),
        cost_estimate=SMALL,
    )(order, frames)


def attention_kernel(first, count_q, slots, state_at, last, k_mask, q_frame, *refs):
    q_parts, kv_parts = refs[:2], refs[2 : 2 + len(slots)]
    rest = refs[2 + len(slots) :]
    queries = count_q * BLOCK
    at = first * BLOCK
    rows_at = pl.ds(at, queries)
    if state_at is not None:
        o_in, log_in = rest[:2]
        rest = rest[2:]
        state_rows = pl.ds(at - state_at * BLOCK, queries)
    out = rest[0]
    hidden = jnp.concatenate(
        [k_mask[pl.ds(n * BLOCK, ref.shape[0]), :] for n, ref in zip(slots, kv_parts)], axis=0
    )
    keys = hidden.shape[0]
    own_frame = q_frame[rows_at, :]
    lane = lax.broadcasted_iota(jnp.int32, (queries, HEAD_DIM), 1)
    ones = jnp.ones((keys, HEAD_DIM), jnp.bfloat16)

    def columns(h, offset=0):
        return pl.ds(offset + h * HEAD_DIM, HEAD_DIM)

    def queries_of(h):
        taken = []
        for part, ref in enumerate(q_parts):
            low, high = max(at - part * 512, 0), min(at + queries - part * 512, 512)
            if low < high:
                taken.append(ref[pl.ds(low, high - low), columns(h)])
        return taken[0] if len(taken) == 1 else jnp.concatenate(taken, axis=0)

    def keys_of(h, offset):
        return jnp.concatenate([ref[:, columns(h, offset)] for ref in kv_parts], axis=0)

    def score(h):
        return lax.dot_general(
            jnp.concatenate([queries_of(h), own_frame], axis=1),
            jnp.concatenate([keys_of(h, 0), hidden], axis=1),
            (((1,), (1,)), ((), ())),
            preferred_element_type=jnp.float32,
        )

    def finish(h, acc, top, logs):
        value, total = acc[:, :HEAD_DIM], acc[:, HEAD_DIM:]
        top = jnp.broadcast_to(top * SCALE, (queries, HEAD_DIM))
        if state_at is not None:
            log = jnp.broadcast_to(log_in[state_rows, pl.ds(h, 1)], (queries, HEAD_DIM))
            both = jnp.maximum(log, top)
            new, old = jnp.exp2(top - both), jnp.exp2(log - both)
            value = value * new + o_in[state_rows, columns(h)] * old
            total = total * new + old
            top = both
        out[:, columns(h)] = (value / total).astype(out.dtype)
        return jnp.where(lane == h, top + jnp.log2(total), logs)

    logs = jnp.zeros((queries, HEAD_DIM), jnp.float32)
    scores, held = score(0), None
    for h in range(HEADS):
        ahead = score(h + 1) if h + 1 < HEADS else None
        top = jnp.max(scores, axis=1, keepdims=True)
        expo = jnp.exp2((scores - top) * SCALE).astype(jnp.bfloat16)
        values = jnp.concatenate([keys_of(h, WIDTH), ones], axis=1)
        acc = jnp.dot(expo, values, preferred_element_type=jnp.float32)
        if held is not None:
            logs = finish(h - 1, *held, logs)
        held, scores = (acc, top), ahead
    logs = finish(HEADS - 1, *held, logs)
    if last:
        out[:, pl.ds(WIDTH, HEAD_DIM)] = three_pieces(logs)
    else:
        rest[1][...] = logs


def attention(blocks, tabled, q_parts, kv_parts, state=(), state_at=0, last=False):
    first, count_q = blocks
    rows = count_q * BLOCK
    if last:
        out_shape = (jax.ShapeDtypeStruct((rows, WIDTH + HEAD_DIM), jnp.bfloat16),)
    else:
        out_shape = (
            jax.ShapeDtypeStruct((rows, WIDTH), jnp.float32),
            jax.ShapeDtypeStruct((rows, HEAD_DIM), jnp.float32),
        )
    slots = tuple(slot for slot, _ in kv_parts)
    return pl.pallas_call(
        functools.partial(
            attention_kernel, first, count_q, slots, state_at if state else None, last
        ),
        out_shape=out_shape,
        in_specs=[VMEM] * (4 + len(kv_parts) + len(state)),
        out_specs=(VMEM,) * len(out_shape),
        compiler_params=pltpu.CompilerParams(vmem_limit_bytes=30 * MIB),
        cost_estimate=SMALL,
    )(*tabled, *q_parts, *(part for _, part in kv_parts), *state)


def merge_kernel(mine, theirs, out):
    logs = []
    for ref in (mine, theirs):
        pieces = ref[:, pl.ds(WIDTH, HEAD_DIM)].astype(jnp.float32)
        logs.append(
            pieces + pltpu.roll(pieces, HEAD_DIM - 8, 1) + pltpu.roll(pieces, HEAD_DIM - 16, 1)
        )
    top = jnp.maximum(logs[0], logs[1])
    first, second = jnp.exp2(logs[0] - top), jnp.exp2(logs[1] - top)
    total = first + second
    first, second = first / total, second / total
    for h in range(HEADS):
        cols = pl.ds(h * HEAD_DIM, HEAD_DIM)
        out[:, cols] = (
            mine[:, cols].astype(jnp.float32) * first[:, h : h + 1]
            + theirs[:, cols].astype(jnp.float32) * second[:, h : h + 1]
        ).astype(jnp.bfloat16)


def merge(mine, theirs, block):
    full = WIDTH + HEAD_DIM
    return pl.pallas_call(
        merge_kernel,
        out_shape=jax.ShapeDtypeStruct((BLOCK, WIDTH), jnp.bfloat16),
        grid=(1,),
        in_specs=[
            pl.BlockSpec((BLOCK, full), lambda i: (block, 0)),
            pl.BlockSpec((BLOCK, full), lambda i: (0, 0)),
        ],
        out_specs=pl.BlockSpec((BLOCK, WIDTH), lambda i: (0, 0)),
        compiler_params=pltpu.CompilerParams(vmem_limit_bytes=8 * MIB),
        cost_estimate=SMALL,
    )(mine, theirs)


def join_kernel(k_ref, v_ref, out_ref, sem):
    copies = [
        pltpu.make_async_copy(ref, out_ref.at[:, pl.ds(n * WIDTH, WIDTH)], sem.at[n])
        for n, ref in enumerate((k_ref, v_ref))
    ]
    for copy in copies:
        copy.start()
    for copy in copies:
        copy.wait()


def join(keys, values):
    return pl.pallas_call(
        join_kernel,
        out_shape=jax.ShapeDtypeStruct((512, 2 * WIDTH), jnp.bfloat16),
        in_specs=[pl.BlockSpec(memory_space=pl.ANY)] * 2,
        out_specs=VMEM,
        scratch_shapes=[pltpu.SemaphoreType.DMA((2,))],
        compiler_params=pltpu.CompilerParams(vmem_limit_bytes=8 * MIB),
        cost_estimate=SMALL,
    )(keys, values)


def project_kernel(give, *refs):
    mine, other, parts, out_ref = refs[:4], refs[4:8], refs[8:13], refs[13]
    core_at, zl_at = lax.axis_index("core"), lax.axis_index("zl")

    def run(weights):
        rows = [
            parts[0][...],
            parts[1][...],
            jnp.concatenate([parts[2][...], parts[3][...]], axis=0),
            parts[4][...],
        ]
        total = None
        for row, w in zip(rows, weights):
            term = jnp.dot(row, w[...], preferred_element_type=jnp.float32)
            total = term if total is None else total + term
        out_ref[...] = total.astype(out_ref.dtype)

    same = core_at == zl_at

    @pl.when(same != give)
    def _():
        run(mine)

    @pl.when(same == give)
    def _():
        run(other)


def project(give, w_mine, w_other, parts, dtype):
    return pl.pallas_call(
        functools.partial(project_kernel, give),
        out_shape=jax.ShapeDtypeStruct((BLOCK, 640), dtype),
        in_specs=[VMEM] * 13,
        out_specs=VMEM,
        compiler_params=pltpu.CompilerParams(vmem_limit_bytes=12 * MIB),
        cost_estimate=SMALL,
    )(*w_mine, *w_other, *parts)


def together(*groups):
    flat, tree = jax.tree.flatten(groups)
    return jax.tree.unflatten(tree, lax.optimization_barrier(tuple(flat)))


def on_device(query, key_rows, value_rows, frame_seq, order, w_out):
    core_at, x_at = lax.axis_index("core"), lax.axis_index("x")

    def columns(zl, distance):
        return lax.dynamic_slice_in_dim(w_out, (zl * 4 + (x_at + distance) % 4) * 640, 640, 1)

    kv = join(key_rows, value_rows)
    kv_next = send(kv, "y", -1)
    kv_back = send(kv, "y", 1)
    q_z = send(query, "zh", 1)
    kv_core = send(kv, "core", 1)
    w_next = send(after(columns(core_at, 3), kv_core), "x", -1)
    w_back = send(after(columns(core_at, 1), kv_core), "x", 1)
    attend = functools.partial(
        attention, tabled=tables(order, frame_seq.reshape(64, 128)), q_parts=(q_z, query)
    )
    state = attend((0, 4), kv_parts=((0, kv), (2, kv_core)))
    kv_next, kv_back, w_next, w_back, state = together(kv_next, kv_back, w_next, w_back, state)

    far_low = send(kv_next[:BLOCK], "y", -1)
    far_high = send(kv_back[BLOCK:], "y", 1)
    next_core = send(kv_next, "core", 1)
    back_core = send(kv_back, "core", 1)
    w_far = send(after(columns(core_at, 2), w_next), "x", 2)
    state = attend((0, 4), kv_parts=((4, kv_next), (6, kv_back)), state=state)
    cores = ((8, next_core), (10, back_core))
    state_z = attend((0, 2), kv_parts=cores, state=state)
    far_low, far_high, state_z = together(far_low, far_high, state_z)

    low_core, high_core = send(far_low, "core", 1), send(far_high, "core", 1)
    w_next_core, w_back_core = send(w_next, "core", 1), send(w_back, "core", 1)
    far = ((12, far_low), (13, far_high))
    state_z = attend((0, 2), kv_parts=far, state=state_z)
    low_core, high_core, w_far, state_z = together(low_core, high_core, w_far, state_z)
    far_core = ((14, low_core), (15, high_core))
    w_far_core = send(w_far, "core", 1)
    got = []
    for block in range(2):
        (give,) = attend((block, 1), kv_parts=far_core, state=state_z, last=True)
        got.append(send(give, "zh", 1))
        state, give = together(state, give)
    state = attend((2, 2), kv_parts=cores, state=state)
    (keep,) = attend((2, 2), kv_parts=far + far_core, state=state, state_at=2, last=True)
    keep, w_next_core, w_back_core, w_far_core = together(
        keep, w_next_core, w_back_core, w_far_core
    )
    w_mine = (columns(core_at, 0), w_next, w_far, w_back)
    w_other = (columns(1 - core_at, 0), w_next_core, w_far_core, w_back_core)

    out = []
    for block, their in enumerate(got):
        done = merge(keep, their, block)
        one, three = send(done, "x", -1), send(done, "x", 1)
        low, high = send(one[:128], "x", -1), send(three[128:], "x", 1)
        out.append([done, one, low, high, three])

    came = [
        send(project(True, w_mine, w_other, parts, jnp.bfloat16), "zl", 1) for parts in out
    ]
    kept = [project(False, w_mine, w_other, parts, jnp.float32) for parts in out]
    return jnp.concatenate(
        [(a + b.astype(jnp.float32)).astype(jnp.bfloat16) for a, b in zip(kept, came)], axis=0
    )


def solution(mesh):
    fine = Mesh(mesh.devices.reshape(4, 2, 2, 2, 4), ("y", "zh", "core", "zl", "x"))
    rows, columns = ("y", "zh", "core"), ("zl", "x")
    return jax.shard_map(
        on_device,
        mesh=fine,
        in_specs=(P(rows, columns),) * 3 + (P(), P(), P(columns, None)),
        out_specs=P(rows, columns),
        check_vma=False,
    )
```

```python
import functools
import math

import jax
import jax.numpy as jnp
from jax import lax
from jax.experimental import pallas as pl
from jax.experimental.pallas import tpu as pltpu
from jax.sharding import Mesh
from jax.sharding import PartitionSpec as P

HEAD_DIM = 128
HEADS = 5
WIDTH = HEADS * HEAD_DIM
BLOCK = 256
FRAMES = 4
BIG = 1e30
SCALE = HEAD_DIM ** (-0.5) * math.log2(math.e)
MIB = 1024 * 1024
TALL = 256
SLOT = {(0, 0): 0, (0, 1): 2, (1, 0): 4, (3, 0): 6, (1, 1): 8, (3, 1): 10, (2, 0): 12, (2, 1): 14}
SMEM = pl.BlockSpec(memory_space=pltpu.SMEM)
VMEM = pl.BlockSpec(memory_space=pltpu.VMEM)
SMALL = pl.CostEstimate(flops=1024, bytes_accessed=1024, transcendentals=0)


def send(value, axis, step):
    size = {"y": 4, "x": 4}.get(axis, 2)
    return lax.ppermute(value, axis, [(i, (i + step) % size) for i in range(size)])


def after(value, *done):
    return lax.optimization_barrier((value, *done))[0]


def three_pieces(value):
    high = value.astype(jnp.bfloat16).astype(jnp.float32)
    rest = value - high
    middle = rest.astype(jnp.bfloat16).astype(jnp.float32)
    low = rest - middle
    return (high + pltpu.roll(middle, 8, 1) + pltpu.roll(low, 16, 1)).astype(jnp.bfloat16)


def tables_kernel(order_ref, frames_ref, k_mask_ref, q_frame_ref):
    y_at, zh_at, core_at = (lax.axis_index(a) for a in ("y", "zh", "core"))
    tokens = order_ref.shape[0] * BLOCK
    ends = []
    for f in range(FRAMES - 1):
        below = jnp.where(frames_ref[...] <= f, 1.0, 0.0)
        ends.append(jnp.sum(below).astype(jnp.int32))
    lane = lax.broadcasted_iota(jnp.int32, (BLOCK, HEAD_DIM), 1)
    offset = lax.broadcasted_iota(jnp.int32, (BLOCK, HEAD_DIM), 0)
    lane_end = jnp.where(
        lane == 0, ends[0], jnp.where(lane == 1, ends[1], jnp.where(lane == 2, ends[2], tokens))
    )
    lane_start = jnp.where(
        lane == 0, 0, jnp.where(lane == 1, ends[0], jnp.where(lane == 2, ends[1], ends[2]))
    )
    for (dy, dc), slot in SLOT.items():
        row = lax.rem(y_at + dy, 4)
        core = 1 - core_at if dc else core_at
        for half in range(2):
            token = order_ref[row * 8 + zh_at * 4 + core * 2 + half] * BLOCK + offset
            hidden = (token >= lane_end) & (lane < FRAMES)
            k_mask_ref[pl.ds((slot + half) * BLOCK, BLOCK), :] = jnp.where(
                hidden, -BIG, 0.0
            ).astype(jnp.bfloat16)
    for n in range(4):
        z = 1 - zh_at if n < 2 else zh_at
        token = order_ref[y_at * 8 + z * 4 + core_at * 2 + n % 2] * BLOCK + offset
        own = (token >= lane_start) & (token < lane_end) & (lane < FRAMES)
        q_frame_ref[pl.ds(n * BLOCK, BLOCK), :] = jnp.where(own, 1.0, 0.0).astype(jnp.bfloat16)


def tables(order, frames):
    return pl.pallas_call(
        tables_kernel,
        out_shape=(
            jax.ShapeDtypeStruct((4096, HEAD_DIM), jnp.bfloat16),
            jax.ShapeDtypeStruct((1024, HEAD_DIM), jnp.bfloat16),
        ),
        in_specs=[SMEM, VMEM],
        out_specs=(VMEM, VMEM),
        compiler_params=pltpu.CompilerParams(vmem_limit_bytes=8 * MIB),
        cost_estimate=SMALL,
    )(order, frames)


def attention_kernel(first, count_q, slots, state_at, last, k_mask, q_frame, *refs):
    q_parts, kv_parts = refs[:2], refs[2 : 2 + len(slots)]
    rest = refs[2 + len(slots) :]
    if state_at is not None:
        o_in, log_in = rest[:2]
        rest = rest[2:]
    out = rest[0]
    part, part_rows = first // 2, (first % 2) * BLOCK
    if count_q > 2:
        queries = rest[-1]
        queries[:512, :] = q_parts[0][...]
        queries[512:, :] = q_parts[1][...]
        part_rows = 0
    else:
        queries = q_parts[part]
    hidden = jnp.concatenate(
        [k_mask[pl.ds(n * BLOCK, ref.shape[0]), :] for n, ref in zip(slots, kv_parts)], axis=0
    )
    keys = hidden.shape[0]
    tall = min(TALL, count_q * BLOCK)
    lane = lax.broadcasted_iota(jnp.int32, (tall, HEAD_DIM), 1)
    ones = jnp.ones((keys, HEAD_DIM), jnp.bfloat16)

    def columns(h, offset=0):
        return pl.ds(offset + h * HEAD_DIM, HEAD_DIM)

    def keys_of(h, offset):
        return jnp.concatenate([ref[:, columns(h, offset)] for ref in kv_parts], axis=0)

    def some_rows(n, carry):
        def rows_from(start):
            return pl.ds(pl.multiple_of(start + n * tall, BLOCK), tall)

        rows = rows_from(0)
        q_rows = rows_from(part_rows)
        own_frame = q_frame[rows_from(first * BLOCK), :]
        if state_at is not None:
            state_rows = rows_from((first - state_at) * BLOCK)

        def score(h):
            return lax.dot_general(
                jnp.concatenate([queries[q_rows, columns(h)], own_frame], axis=1),
                jnp.concatenate([keys_of(h, 0), hidden], axis=1),
                (((1,), (1,)), ((), ())),
                preferred_element_type=jnp.float32,
            )

        def finish(h, acc, top, logs):
            value, total = acc[:, :HEAD_DIM], acc[:, HEAD_DIM:]
            top = jnp.broadcast_to(top * SCALE, (tall, HEAD_DIM))
            if state_at is not None:
                log = jnp.broadcast_to(log_in[state_rows, pl.ds(h, 1)], (tall, HEAD_DIM))
                both = jnp.maximum(log, top)
                new, old = jnp.exp2(top - both), jnp.exp2(log - both)
                value = value * new + o_in[state_rows, columns(h)] * old
                total = total * new + old
                top = both
            out[rows, columns(h)] = (value / total).astype(out.dtype)
            return jnp.where(lane == h, top + jnp.log2(total), logs)

        logs = jnp.zeros((tall, HEAD_DIM), jnp.float32)
        scores, held = score(0), None
        for h in range(HEADS):
            ahead = score(h + 1) if h + 1 < HEADS else None
            top = jnp.max(scores, axis=1, keepdims=True)
            expo = jnp.exp2((scores - top) * SCALE).astype(jnp.bfloat16)
            values = jnp.concatenate([keys_of(h, WIDTH), ones], axis=1)
            acc = jnp.dot(expo, values, preferred_element_type=jnp.float32)
            if held is not None:
                logs = finish(h - 1, *held, logs)
            held, scores = (acc, top), ahead
        logs = finish(HEADS - 1, *held, logs)
        if last:
            out[rows, pl.ds(WIDTH, HEAD_DIM)] = three_pieces(logs)
        else:
            rest[1][rows, :] = logs
        return carry

    lax.fori_loop(0, count_q * BLOCK // tall, some_rows, 0)


def attention(blocks, tabled, q_parts, kv_parts, state=(), state_at=0, last=False):
    first, count_q = blocks
    rows = count_q * BLOCK
    if last:
        out_shape = (jax.ShapeDtypeStruct((rows, WIDTH + HEAD_DIM), jnp.bfloat16),)
    else:
        out_shape = (
            jax.ShapeDtypeStruct((rows, WIDTH), jnp.float32),
            jax.ShapeDtypeStruct((rows, HEAD_DIM), jnp.float32),
        )
    slots = tuple(slot for slot, _ in kv_parts)
    return pl.pallas_call(
        functools.partial(
            attention_kernel, first, count_q, slots, state_at if state else None, last
        ),
        out_shape=out_shape,
        in_specs=[VMEM] * (4 + len(kv_parts) + len(state)),
        out_specs=(VMEM,) * len(out_shape),
        scratch_shapes=[pltpu.VMEM((rows, WIDTH), jnp.bfloat16)] if count_q > 2 else [],
        compiler_params=pltpu.CompilerParams(vmem_limit_bytes=30 * MIB),
        cost_estimate=SMALL,
    )(*tabled, *q_parts, *(part for _, part in kv_parts), *state)


def merge_kernel(mine, theirs, out):
    logs = []
    for ref in (mine, theirs):
        pieces = ref[:, pl.ds(WIDTH, HEAD_DIM)].astype(jnp.float32)
        logs.append(
            pieces + pltpu.roll(pieces, HEAD_DIM - 8, 1) + pltpu.roll(pieces, HEAD_DIM - 16, 1)
        )
    top = jnp.maximum(logs[0], logs[1])
    first, second = jnp.exp2(logs[0] - top), jnp.exp2(logs[1] - top)
    total = first + second
    first, second = first / total, second / total
    for h in range(HEADS):
        cols = pl.ds(h * HEAD_DIM, HEAD_DIM)
        out[:, cols] = (
            mine[:, cols].astype(jnp.float32) * first[:, h : h + 1]
            + theirs[:, cols].astype(jnp.float32) * second[:, h : h + 1]
        ).astype(jnp.bfloat16)


def merge(mine, theirs, block):
    full = WIDTH + HEAD_DIM
    return pl.pallas_call(
        merge_kernel,
        out_shape=jax.ShapeDtypeStruct((BLOCK, WIDTH), jnp.bfloat16),
        grid=(1,),
        in_specs=[
            pl.BlockSpec((BLOCK, full), lambda i: (block, 0)),
            pl.BlockSpec((BLOCK, full), lambda i: (0, 0)),
        ],
        out_specs=pl.BlockSpec((BLOCK, WIDTH), lambda i: (0, 0)),
        compiler_params=pltpu.CompilerParams(vmem_limit_bytes=8 * MIB),
        cost_estimate=SMALL,
    )(mine, theirs)


def join_kernel(k_ref, v_ref, out_ref, sem):
    copies = [
        pltpu.make_async_copy(ref, out_ref.at[:, pl.ds(n * WIDTH, WIDTH)], sem.at[n])
        for n, ref in enumerate((k_ref, v_ref))
    ]
    for copy in copies:
        copy.start()
    for copy in copies:
        copy.wait()


def join(keys, values):
    return pl.pallas_call(
        join_kernel,
        out_shape=jax.ShapeDtypeStruct((512, 2 * WIDTH), jnp.bfloat16),
        in_specs=[pl.BlockSpec(memory_space=pl.ANY)] * 2,
        out_specs=VMEM,
        scratch_shapes=[pltpu.SemaphoreType.DMA((2,))],
        compiler_params=pltpu.CompilerParams(vmem_limit_bytes=8 * MIB),
        cost_estimate=SMALL,
    )(keys, values)


def project_kernel(give, *refs):
    mine, other, parts, out_ref = refs[:4], refs[4:8], refs[8:13], refs[13]
    core_at, zl_at = lax.axis_index("core"), lax.axis_index("zl")

    def run(weights):
        rows = [
            parts[0][...],
            parts[1][...],
            jnp.concatenate([parts[2][...], parts[3][...]], axis=0),
            parts[4][...],
        ]
        total = None
        for row, w in zip(rows, weights):
            term = jnp.dot(row, w[...], preferred_element_type=jnp.float32)
            total = term if total is None else total + term
        out_ref[...] = total.astype(out_ref.dtype)

    same = core_at == zl_at

    @pl.when(same != give)
    def _():
        run(mine)

    @pl.when(same == give)
    def _():
        run(other)


def project(give, w_mine, w_other, parts, dtype):
    return pl.pallas_call(
        functools.partial(project_kernel, give),
        out_shape=jax.ShapeDtypeStruct((BLOCK, 640), dtype),
        in_specs=[VMEM] * 13,
        out_specs=VMEM,
        compiler_params=pltpu.CompilerParams(vmem_limit_bytes=12 * MIB),
        cost_estimate=SMALL,
    )(*w_mine, *w_other, *parts)


def together(*groups):
    flat, tree = jax.tree.flatten(groups)
    return jax.tree.unflatten(tree, lax.optimization_barrier(tuple(flat)))


def on_device(query, key_rows, value_rows, frame_seq, order, w_out):
    core_at, x_at = lax.axis_index("core"), lax.axis_index("x")

    def columns(zl, distance):
        return lax.dynamic_slice_in_dim(w_out, (zl * 4 + (x_at + distance) % 4) * 640, 640, 1)

    kv = join(key_rows, value_rows)
    kv_next = send(kv, "y", -1)
    kv_back = send(kv, "y", 1)
    q_z = send(query, "zh", 1)
    kv_core = send(kv, "core", 1)
    w_next = send(after(columns(core_at, 3), kv_core), "x", -1)
    w_back = send(after(columns(core_at, 1), kv_core), "x", 1)
    attend = functools.partial(
        attention, tabled=tables(order, frame_seq.reshape(64, 128)), q_parts=(q_z, query)
    )
    state = attend((0, 4), kv_parts=((0, kv), (2, kv_core)))
    kv_next, kv_back, w_next, w_back, state = together(kv_next, kv_back, w_next, w_back, state)

    far_low = send(kv_next[:BLOCK], "y", -1)
    far_high = send(kv_back[BLOCK:], "y", 1)
    next_core = send(kv_next, "core", 1)
    back_core = send(kv_back, "core", 1)
    w_far = send(after(columns(core_at, 2), w_next), "x", 2)
    state = attend((0, 4), kv_parts=((4, kv_next), (6, kv_back)), state=state)
    cores = ((8, next_core), (10, back_core))
    state_z = attend((0, 2), kv_parts=cores, state=state)
    far_low, far_high, state_z = together(far_low, far_high, state_z)

    low_core, high_core = send(far_low, "core", 1), send(far_high, "core", 1)
    w_next_core, w_back_core = send(w_next, "core", 1), send(w_back, "core", 1)
    far = ((12, far_low), (13, far_high))
    state_z = attend((0, 2), kv_parts=far, state=state_z)
    low_core, high_core, w_far, state_z = together(low_core, high_core, w_far, state_z)
    far_core = ((14, low_core), (15, high_core))
    w_far_core = send(w_far, "core", 1)
    got = []
    for block in range(2):
        (give,) = attend((block, 1), kv_parts=far_core, state=state_z, last=True)
        got.append(send(give, "zh", 1))
        state, give = together(state, give)
    state = attend((2, 2), kv_parts=cores, state=state)
    (keep,) = attend((2, 2), kv_parts=far + far_core, state=state, state_at=2, last=True)
    keep, w_next_core, w_back_core, w_far_core = together(
        keep, w_next_core, w_back_core, w_far_core
    )
    w_mine = (columns(core_at, 0), w_next, w_far, w_back)
    w_other = (columns(1 - core_at, 0), w_next_core, w_far_core, w_back_core)

    out = []
    for block, their in enumerate(got):
        done = merge(keep, their, block)
        one, three = send(done, "x", -1), send(done, "x", 1)
        low, high = send(one[:128], "x", -1), send(three[128:], "x", 1)
        out.append([done, one, low, high, three])

    came = [
        send(project(True, w_mine, w_other, parts, jnp.bfloat16), "zl", 1) for parts in out
    ]
    kept = [project(False, w_mine, w_other, parts, jnp.float32) for parts in out]
    return jnp.concatenate(
        [(a + b.astype(jnp.float32)).astype(jnp.bfloat16) for a, b in zip(kept, came)], axis=0
    )


def solution(mesh):
    fine = Mesh(mesh.devices.reshape(4, 2, 2, 2, 4), ("y", "zh", "core", "zl", "x"))
    rows, columns = ("y", "zh", "core"), ("zl", "x")
    return jax.shard_map(
        on_device,
        mesh=fine,
        in_specs=(P(rows, columns),) * 3 + (P(), P(), P(columns, None)),
        out_specs=P(rows, columns),
        check_vma=False,
    )
```

```python
import functools
import math

import jax
import jax.numpy as jnp
from jax import lax
from jax.experimental import pallas as pl
from jax.experimental.pallas import tpu as pltpu
from jax.sharding import Mesh
from jax.sharding import PartitionSpec as P

HEAD_DIM = 128
HEADS = 5
WIDTH = HEADS * HEAD_DIM
BLOCK = 256
FRAMES = 4
BIG = 1e30
SCALE = HEAD_DIM ** (-0.5) * math.log2(math.e)
MIB = 1024 * 1024
TALL = 256
SLOT = {(0, 0): 0, (0, 1): 2, (1, 0): 4, (3, 0): 6, (1, 1): 8, (3, 1): 10, (2, 0): 12, (2, 1): 14}
SMEM = pl.BlockSpec(memory_space=pltpu.SMEM)
VMEM = pl.BlockSpec(memory_space=pltpu.VMEM)
SMALL = pl.CostEstimate(flops=1024, bytes_accessed=1024, transcendentals=0)


def send(value, axis, step):
    size = {"y": 4, "x": 4}.get(axis, 2)
    return lax.ppermute(value, axis, [(i, (i + step) % size) for i in range(size)])


def after(value, *done):
    return lax.optimization_barrier((value, *done))[0]


def three_pieces(value):
    high = value.astype(jnp.bfloat16).astype(jnp.float32)
    rest = value - high
    middle = rest.astype(jnp.bfloat16).astype(jnp.float32)
    low = rest - middle
    return (high + pltpu.roll(middle, 8, 1) + pltpu.roll(low, 16, 1)).astype(jnp.bfloat16)


def tables_kernel(order_ref, frames_ref, k_mask_ref, q_frame_ref):
    y_at, zh_at, core_at = (lax.axis_index(a) for a in ("y", "zh", "core"))
    tokens = order_ref.shape[0] * BLOCK
    ends = []
    for f in range(FRAMES - 1):
        below = jnp.where(frames_ref[...] <= f, 1.0, 0.0)
        ends.append(jnp.sum(below).astype(jnp.int32))
    lane = lax.broadcasted_iota(jnp.int32, (BLOCK, HEAD_DIM), 1)
    offset = lax.broadcasted_iota(jnp.int32, (BLOCK, HEAD_DIM), 0)
    lane_end = jnp.where(
        lane == 0, ends[0], jnp.where(lane == 1, ends[1], jnp.where(lane == 2, ends[2], tokens))
    )
    lane_start = jnp.where(
        lane == 0, 0, jnp.where(lane == 1, ends[0], jnp.where(lane == 2, ends[1], ends[2]))
    )
    for (dy, dc), slot in SLOT.items():
        row = lax.rem(y_at + dy, 4)
        core = 1 - core_at if dc else core_at
        for half in range(2):
            token = order_ref[row * 8 + zh_at * 4 + core * 2 + half] * BLOCK + offset
            hidden = (token >= lane_end) & (lane < FRAMES)
            k_mask_ref[pl.ds((slot + half) * BLOCK, BLOCK), :] = jnp.where(
                hidden, -BIG, 0.0
            ).astype(jnp.bfloat16)
    for n in range(4):
        z = 1 - zh_at if n < 2 else zh_at
        token = order_ref[y_at * 8 + z * 4 + core_at * 2 + n % 2] * BLOCK + offset
        own = (token >= lane_start) & (token < lane_end) & (lane < FRAMES)
        q_frame_ref[pl.ds(n * BLOCK, BLOCK), :] = jnp.where(own, 1.0, 0.0).astype(jnp.bfloat16)


def tables(order, frames):
    return pl.pallas_call(
        tables_kernel,
        out_shape=(
            jax.ShapeDtypeStruct((4096, HEAD_DIM), jnp.bfloat16),
            jax.ShapeDtypeStruct((1024, HEAD_DIM), jnp.bfloat16),
        ),
        in_specs=[SMEM, VMEM],
        out_specs=(VMEM, VMEM),
        compiler_params=pltpu.CompilerParams(vmem_limit_bytes=8 * MIB),
        cost_estimate=SMALL,
    )(order, frames)


def attention_kernel(first, count_q, slots, state_at, last, k_mask, q_frame, *refs):
    queries, kv_parts = refs[0], refs[1 : 1 + len(slots)]
    rest = refs[1 + len(slots) :]
    if state_at is not None:
        o_in, log_in = rest[:2]
        rest = rest[2:]
    out = rest[0]
    part_rows = (first % 2) * BLOCK
    hidden = jnp.concatenate(
        [k_mask[pl.ds(n * BLOCK, ref.shape[0]), :] for n, ref in zip(slots, kv_parts)], axis=0
    )
    keys = hidden.shape[0]
    tall = min(TALL, count_q * BLOCK)
    lane = lax.broadcasted_iota(jnp.int32, (tall, HEAD_DIM), 1)
    ones = jnp.ones((keys, HEAD_DIM), jnp.bfloat16)

    def columns(h, offset=0):
        return pl.ds(offset + h * HEAD_DIM, HEAD_DIM)

    def keys_of(h, offset):
        return jnp.concatenate([ref[:, columns(h, offset)] for ref in kv_parts], axis=0)

    def some_rows(n, carry):
        def rows_from(start):
            return pl.ds(pl.multiple_of(start + n * tall, BLOCK), tall)

        rows = rows_from(0)
        q_rows = rows_from(part_rows)
        own_frame = q_frame[rows_from(first * BLOCK), :]
        if state_at is not None:
            state_rows = rows_from((first - state_at) * BLOCK)

        def score(h):
            return lax.dot_general(
                jnp.concatenate([queries[q_rows, columns(h)], own_frame], axis=1),
                jnp.concatenate([keys_of(h, 0), hidden], axis=1),
                (((1,), (1,)), ((), ())),
                preferred_element_type=jnp.float32,
            )

        def finish(h, acc, top, logs):
            value, total = acc[:, :HEAD_DIM], acc[:, HEAD_DIM:]
            top = jnp.broadcast_to(top * SCALE, (tall, HEAD_DIM))
            if state_at is not None:
                log = jnp.broadcast_to(log_in[state_rows, pl.ds(h, 1)], (tall, HEAD_DIM))
                both = jnp.maximum(log, top)
                new, old = jnp.exp2(top - both), jnp.exp2(log - both)
                value = value * new + o_in[state_rows, columns(h)] * old
                total = total * new + old
                top = both
            out[rows, columns(h)] = (value / total).astype(out.dtype)
            return jnp.where(lane == h, top + jnp.log2(total), logs)

        logs = jnp.zeros((tall, HEAD_DIM), jnp.float32)
        scores, held = score(0), None
        for h in range(HEADS):
            ahead = score(h + 1) if h + 1 < HEADS else None
            top = jnp.max(scores, axis=1, keepdims=True)
            expo = jnp.exp2((scores - top) * SCALE).astype(jnp.bfloat16)
            values = jnp.concatenate([keys_of(h, WIDTH), ones], axis=1)
            acc = jnp.dot(expo, values, preferred_element_type=jnp.float32)
            if held is not None:
                logs = finish(h - 1, *held, logs)
            held, scores = (acc, top), ahead
        logs = finish(HEADS - 1, *held, logs)
        if last:
            out[rows, pl.ds(WIDTH, HEAD_DIM)] = three_pieces(logs)
        else:
            rest[1][rows, :] = logs
        return carry

    lax.fori_loop(0, count_q * BLOCK // tall, some_rows, 0)


def attention(blocks, tabled, q_parts, kv_parts, state=(), state_at=0, last=False):
    first, count_q = blocks
    rows = count_q * BLOCK
    if last:
        out_shape = (jax.ShapeDtypeStruct((rows, WIDTH + HEAD_DIM), jnp.bfloat16),)
    else:
        out_shape = (
            jax.ShapeDtypeStruct((rows, WIDTH), jnp.float32),
            jax.ShapeDtypeStruct((rows, HEAD_DIM), jnp.float32),
        )
    slots = tuple(slot for slot, _ in kv_parts)
    return pl.pallas_call(
        functools.partial(
            attention_kernel, first, count_q, slots, state_at if state else None, last
        ),
        out_shape=out_shape,
        in_specs=[VMEM] * (3 + len(kv_parts) + len(state)),
        out_specs=(VMEM,) * len(out_shape),
        compiler_params=pltpu.CompilerParams(vmem_limit_bytes=30 * MIB),
        cost_estimate=SMALL,
    )(*tabled, q_parts[first // 2], *(part for _, part in kv_parts), *state)


def merge_kernel(mine, theirs, out):
    logs = []
    for ref in (mine, theirs):
        pieces = ref[:, pl.ds(WIDTH, HEAD_DIM)].astype(jnp.float32)
        logs.append(
            pieces + pltpu.roll(pieces, HEAD_DIM - 8, 1) + pltpu.roll(pieces, HEAD_DIM - 16, 1)
        )
    top = jnp.maximum(logs[0], logs[1])
    first, second = jnp.exp2(logs[0] - top), jnp.exp2(logs[1] - top)
    total = first + second
    first, second = first / total, second / total
    for h in range(HEADS):
        cols = pl.ds(h * HEAD_DIM, HEAD_DIM)
        out[:, cols] = (
            mine[:, cols].astype(jnp.float32) * first[:, h : h + 1]
            + theirs[:, cols].astype(jnp.float32) * second[:, h : h + 1]
        ).astype(jnp.bfloat16)


def merge(mine, theirs, block):
    full = WIDTH + HEAD_DIM
    return pl.pallas_call(
        merge_kernel,
        out_shape=jax.ShapeDtypeStruct((BLOCK, WIDTH), jnp.bfloat16),
        grid=(1,),
        in_specs=[
            pl.BlockSpec((BLOCK, full), lambda i: (block, 0)),
            pl.BlockSpec((BLOCK, full), lambda i: (0, 0)),
        ],
        out_specs=pl.BlockSpec((BLOCK, WIDTH), lambda i: (0, 0)),
        compiler_params=pltpu.CompilerParams(vmem_limit_bytes=8 * MIB),
        cost_estimate=SMALL,
    )(mine, theirs)


def join_kernel(k_ref, v_ref, out_ref, sem):
    copies = [
        pltpu.make_async_copy(ref, out_ref.at[:, pl.ds(n * WIDTH, WIDTH)], sem.at[n])
        for n, ref in enumerate((k_ref, v_ref))
    ]
    for copy in copies:
        copy.start()
    for copy in copies:
        copy.wait()


def join(keys, values):
    return pl.pallas_call(
        join_kernel,
        out_shape=jax.ShapeDtypeStruct((512, 2 * WIDTH), jnp.bfloat16),
        in_specs=[pl.BlockSpec(memory_space=pl.ANY)] * 2,
        out_specs=VMEM,
        scratch_shapes=[pltpu.SemaphoreType.DMA((2,))],
        compiler_params=pltpu.CompilerParams(vmem_limit_bytes=8 * MIB),
        cost_estimate=SMALL,
    )(*(pltpu.with_memory_space_constraint(a, pltpu.HBM) for a in (keys, values)))


def project_kernel(give, *refs):
    mine, other, parts, out_ref, far = refs[:4], refs[4:8], refs[8:13], refs[13], refs[14]
    far[:128, :] = parts[2][...]
    far[128:, :] = parts[3][...]
    core_at, zl_at = lax.axis_index("core"), lax.axis_index("zl")

    def run(weights):
        def half(n, carry):
            rows = pl.ds(pl.multiple_of(n * 128, 128), 128)
            total = None
            for part, w in zip((parts[0], parts[1], far, parts[4]), weights):
                term = jnp.dot(part[rows, :], w[...], preferred_element_type=jnp.float32)
                total = term if total is None else total + term
            out_ref[rows, :] = total.astype(out_ref.dtype)
            return carry

        lax.fori_loop(0, 2, half, 0)

    same = core_at == zl_at

    @pl.when(same != give)
    def _():
        run(mine)

    @pl.when(same == give)
    def _():
        run(other)


def project(give, w_mine, w_other, parts, dtype):
    return pl.pallas_call(
        functools.partial(project_kernel, give),
        out_shape=jax.ShapeDtypeStruct((BLOCK, 640), dtype),
        in_specs=[VMEM] * 13,
        out_specs=VMEM,
        scratch_shapes=[pltpu.VMEM((BLOCK, WIDTH), jnp.bfloat16)],
        compiler_params=pltpu.CompilerParams(vmem_limit_bytes=12 * MIB),
        cost_estimate=SMALL,
    )(*w_mine, *w_other, *parts)


def together(*groups):
    flat, tree = jax.tree.flatten(groups)
    return jax.tree.unflatten(tree, lax.optimization_barrier(tuple(flat)))


def on_device(query, key_rows, value_rows, frame_seq, order, w_out):
    core_at, x_at = lax.axis_index("core"), lax.axis_index("x")

    def columns(zl, distance):
        return lax.dynamic_slice_in_dim(w_out, (zl * 4 + (x_at + distance) % 4) * 640, 640, 1)

    kv = join(key_rows, value_rows)
    kv_next = send(kv, "y", -1)
    kv_back = send(kv, "y", 1)
    q_z = send(query, "zh", 1)
    kv_core = send(kv, "core", 1)
    w_next = send(after(columns(core_at, 3), kv_core), "x", -1)
    w_back = send(after(columns(core_at, 1), kv_core), "x", 1)
    tabled = tables(order, frame_seq.reshape(64, 128))

    def attend(blocks, **named):
        return attention(blocks, tabled, (q_z, query), **named)

    near = ((0, kv), (2, kv_core))
    state = attend((2, 2), kv_parts=near)
    q_z, state = together(q_z, state)
    state_z = attend((0, 2), kv_parts=near)
    kv_next, kv_back, w_next, w_back, state, state_z = together(
        kv_next, kv_back, w_next, w_back, state, state_z
    )

    far_low = send(kv_next[:BLOCK], "y", -1)
    far_high = send(kv_back[BLOCK:], "y", 1)
    next_core = send(kv_next, "core", 1)
    back_core = send(kv_back, "core", 1)
    w_far = send(after(columns(core_at, 2), w_next), "x", 2)
    near = ((4, kv_next), (6, kv_back))
    cores = ((8, next_core), (10, back_core))
    state_z = attend((0, 2), kv_parts=near + cores, state=state_z)
    state, state_z = together(state, state_z)
    state = attend((2, 2), kv_parts=near, state=state, state_at=2)
    far_low, far_high, state_z, state = together(far_low, far_high, state_z, state)

    low_core, high_core = send(far_low, "core", 1), send(far_high, "core", 1)
    w_next_core, w_back_core = send(w_next, "core", 1), send(w_back, "core", 1)
    far = ((12, far_low), (13, far_high))
    state_z = attend((0, 2), kv_parts=far, state=state_z)
    low_core, high_core, w_far, state_z = together(low_core, high_core, w_far, state_z)
    far_core = ((14, low_core), (15, high_core))
    w_far_core = send(w_far, "core", 1)
    got = []
    for block in range(2):
        (give,) = attend((block, 1), kv_parts=far_core, state=state_z, last=True)
        got.append(send(give, "zh", 1))
        state, give = together(state, give)
    state = attend((2, 2), kv_parts=cores, state=state, state_at=2)
    (keep,) = attend((2, 2), kv_parts=far + far_core, state=state, state_at=2, last=True)
    keep, w_next_core, w_back_core, w_far_core = together(
        keep, w_next_core, w_back_core, w_far_core
    )
    w_mine = (columns(core_at, 0), w_next, w_far, w_back)
    w_other = (columns(1 - core_at, 0), w_next_core, w_far_core, w_back_core)

    out = []
    for block, their in enumerate(got):
        done = merge(keep, their, block)
        one, three = send(done, "x", -1), send(done, "x", 1)
        low, high = send(one[:128], "x", -1), send(three[128:], "x", 1)
        out.append([done, one, low, high, three])

    came = [
        send(project(True, w_mine, w_other, parts, jnp.bfloat16), "zl", 1) for parts in out
    ]
    kept = [project(False, w_mine, w_other, parts, jnp.float32) for parts in out]
    return jnp.concatenate(
        [(a + b.astype(jnp.float32)).astype(jnp.bfloat16) for a, b in zip(kept, came)], axis=0
    )


def solution(mesh):
    fine = Mesh(mesh.devices.reshape(4, 2, 2, 2, 4), ("y", "zh", "core", "zl", "x"))
    rows, columns = ("y", "zh", "core"), ("zl", "x")
    return jax.shard_map(
        on_device,
        mesh=fine,
        in_specs=(P(rows, columns),) * 3 + (P(), P(), P(columns, None)),
        out_specs=P(rows, columns),
        check_vma=False,
    )
```

```python
import functools
import math

import jax
import jax.numpy as jnp
from jax import lax
from jax.experimental import pallas as pl
from jax.experimental.pallas import tpu as pltpu
from jax.sharding import Mesh
from jax.sharding import PartitionSpec as P

HEAD_DIM = 128
HEADS = 5
WIDTH = HEADS * HEAD_DIM
BLOCK = 256
FRAMES = 4
BIG = 1e30
SCALE = HEAD_DIM ** (-0.5) * math.log2(math.e)
MIB = 1024 * 1024
SLOT = {(0, 0): 0, (0, 1): 2, (1, 0): 4, (3, 0): 6, (1, 1): 8, (3, 1): 10, (2, 0): 12, (2, 1): 14}
SMEM = pl.BlockSpec(memory_space=pltpu.SMEM)
VMEM = pl.BlockSpec(memory_space=pltpu.VMEM)
SMALL = pl.CostEstimate(flops=1024, bytes_accessed=1024, transcendentals=0)


def send(value, axis, step):
    size = {"y": 4, "x": 4}.get(axis, 2)
    return lax.ppermute(value, axis, [(i, (i + step) % size) for i in range(size)])


def after(value, *done):
    return lax.optimization_barrier((value, *done))[0]


def three_pieces(value):
    high = value.astype(jnp.bfloat16).astype(jnp.float32)
    rest = value - high
    middle = rest.astype(jnp.bfloat16).astype(jnp.float32)
    low = rest - middle
    return (high + pltpu.roll(middle, 8, 1) + pltpu.roll(low, 16, 1)).astype(jnp.bfloat16)


def tables_kernel(order_ref, frames_ref, k_mask_ref, q_frame_ref):
    y_at, zh_at, core_at = (lax.axis_index(a) for a in ("y", "zh", "core"))
    tokens = order_ref.shape[0] * BLOCK
    ends = []
    for f in range(FRAMES - 1):
        below = jnp.where(frames_ref[...] <= f, 1.0, 0.0)
        ends.append(jnp.sum(below).astype(jnp.int32))
    lane = lax.broadcasted_iota(jnp.int32, (BLOCK, HEAD_DIM), 1)
    offset = lax.broadcasted_iota(jnp.int32, (BLOCK, HEAD_DIM), 0)
    lane_end = jnp.where(
        lane == 0, ends[0], jnp.where(lane == 1, ends[1], jnp.where(lane == 2, ends[2], tokens))
    )
    lane_start = jnp.where(
        lane == 0, 0, jnp.where(lane == 1, ends[0], jnp.where(lane == 2, ends[1], ends[2]))
    )
    for (dy, dc), slot in SLOT.items():
        row = lax.rem(y_at + dy, 4)
        core = 1 - core_at if dc else core_at
        for half in range(2):
            token = order_ref[row * 8 + zh_at * 4 + core * 2 + half] * BLOCK + offset
            hidden = (token >= lane_end) & (lane < FRAMES)
            k_mask_ref[pl.ds((slot + half) * BLOCK, BLOCK), :] = jnp.where(
                hidden, -BIG, 0.0
            ).astype(jnp.bfloat16)
    for n in range(4):
        z = 1 - zh_at if n < 2 else zh_at
        token = order_ref[y_at * 8 + z * 4 + core_at * 2 + n % 2] * BLOCK + offset
        own = (token >= lane_start) & (token < lane_end) & (lane < FRAMES)
        q_frame_ref[pl.ds(n * BLOCK, BLOCK), :] = jnp.where(own, 1.0, 0.0).astype(jnp.bfloat16)


def tables(order, frames):
    return pl.pallas_call(
        tables_kernel,
        out_shape=(
            jax.ShapeDtypeStruct((4096, HEAD_DIM), jnp.bfloat16),
            jax.ShapeDtypeStruct((1024, HEAD_DIM), jnp.bfloat16),
        ),
        in_specs=[SMEM, VMEM],
        out_specs=(VMEM, VMEM),
        compiler_params=pltpu.CompilerParams(vmem_limit_bytes=8 * MIB),
        cost_estimate=SMALL,
    )(order, frames)


def attention_kernel(first, count_q, slots, state_at, last, tall, k_mask, q_frame, *refs):
    queries, kv_parts = refs[0], refs[1 : 1 + len(slots)]
    rest = refs[1 + len(slots) :]
    if state_at is not None:
        o_in, log_in = rest[:2]
        rest = rest[2:]
    out = rest[0]
    part_rows = (first % 2) * BLOCK
    hidden = jnp.concatenate(
        [k_mask[pl.ds(n * BLOCK, ref.shape[0]), :] for n, ref in zip(slots, kv_parts)], axis=0
    )
    keys = hidden.shape[0]
    lane = lax.broadcasted_iota(jnp.int32, (tall, HEAD_DIM), 1)
    ones = jnp.ones((keys, HEAD_DIM), jnp.bfloat16)

    def columns(h, offset=0):
        return pl.ds(offset + h * HEAD_DIM, HEAD_DIM)

    def keys_of(h, offset):
        return jnp.concatenate([ref[:, columns(h, offset)] for ref in kv_parts], axis=0)

    def some_rows(n, carry):
        def rows_from(start):
            return pl.ds(pl.multiple_of(start + n * tall, BLOCK), tall)

        rows = rows_from(0)
        q_rows = rows_from(part_rows)
        own_frame = q_frame[rows_from(first * BLOCK), :]
        if state_at is not None:
            state_rows = rows_from((first - state_at) * BLOCK)

        def score(h):
            return lax.dot_general(
                jnp.concatenate([queries[q_rows, columns(h)], own_frame], axis=1),
                jnp.concatenate([keys_of(h, 0), hidden], axis=1),
                (((1,), (1,)), ((), ())),
                preferred_element_type=jnp.float32,
            )

        def finish(h, acc, top, logs):
            value, total = acc[:, :HEAD_DIM], acc[:, HEAD_DIM:]
            top = jnp.broadcast_to(top * SCALE, (tall, HEAD_DIM))
            if state_at is not None:
                log = jnp.broadcast_to(log_in[state_rows, pl.ds(h, 1)], (tall, HEAD_DIM))
                both = jnp.maximum(log, top)
                new, old = jnp.exp2(top - both), jnp.exp2(log - both)
                value = value * new + o_in[state_rows, columns(h)] * old
                total = total * new + old
                top = both
            out[rows, columns(h)] = (value / total).astype(out.dtype)
            return jnp.where(lane == h, top + jnp.log2(total), logs)

        logs = jnp.zeros((tall, HEAD_DIM), jnp.float32)
        scores, held = score(0), None
        for h in range(HEADS):
            ahead = score(h + 1) if h + 1 < HEADS else None
            top = jnp.max(scores, axis=1, keepdims=True)
            expo = jnp.exp2((scores - top) * SCALE).astype(jnp.bfloat16)
            values = jnp.concatenate([keys_of(h, WIDTH), ones], axis=1)
            acc = jnp.dot(expo, values, preferred_element_type=jnp.float32)
            if held is not None:
                logs = finish(h - 1, *held, logs)
            held, scores = (acc, top), ahead
        logs = finish(HEADS - 1, *held, logs)
        if last:
            out[rows, pl.ds(WIDTH, HEAD_DIM)] = three_pieces(logs)
        else:
            rest[1][rows, :] = logs
        return carry

    lax.fori_loop(0, count_q * BLOCK // tall, some_rows, 0)


def attention(blocks, tabled, q_parts, kv_parts, state=(), state_at=0, last=False, tall=BLOCK):
    first, count_q = blocks
    rows = count_q * BLOCK
    if last:
        out_shape = (jax.ShapeDtypeStruct((rows, WIDTH + HEAD_DIM), jnp.bfloat16),)
    else:
        out_shape = (
            jax.ShapeDtypeStruct((rows, WIDTH), jnp.float32),
            jax.ShapeDtypeStruct((rows, HEAD_DIM), jnp.float32),
        )
    slots = tuple(slot for slot, _ in kv_parts)
    return pl.pallas_call(
        functools.partial(
            attention_kernel, first, count_q, slots, state_at if state else None, last, tall
        ),
        out_shape=out_shape,
        in_specs=[VMEM] * (3 + len(kv_parts) + len(state)),
        out_specs=(VMEM,) * len(out_shape),
        compiler_params=pltpu.CompilerParams(vmem_limit_bytes=30 * MIB),
        cost_estimate=SMALL,
    )(*tabled, q_parts[first // 2], *(part for _, part in kv_parts), *state)


def merge_kernel(mine, theirs, out):
    logs = []
    for ref in (mine, theirs):
        pieces = ref[:, pl.ds(WIDTH, HEAD_DIM)].astype(jnp.float32)
        logs.append(
            pieces + pltpu.roll(pieces, HEAD_DIM - 8, 1) + pltpu.roll(pieces, HEAD_DIM - 16, 1)
        )
    top = jnp.maximum(logs[0], logs[1])
    first, second = jnp.exp2(logs[0] - top), jnp.exp2(logs[1] - top)
    total = first + second
    first, second = first / total, second / total
    for h in range(HEADS):
        cols = pl.ds(h * HEAD_DIM, HEAD_DIM)
        out[:, cols] = (
            mine[:, cols].astype(jnp.float32) * first[:, h : h + 1]
            + theirs[:, cols].astype(jnp.float32) * second[:, h : h + 1]
        ).astype(jnp.bfloat16)


def merge(mine, theirs, block):
    full = WIDTH + HEAD_DIM
    return pl.pallas_call(
        merge_kernel,
        out_shape=jax.ShapeDtypeStruct((BLOCK, WIDTH), jnp.bfloat16),
        grid=(1,),
        in_specs=[
            pl.BlockSpec((BLOCK, full), lambda i: (block, 0)),
            pl.BlockSpec((BLOCK, full), lambda i: (0, 0)),
        ],
        out_specs=pl.BlockSpec((BLOCK, WIDTH), lambda i: (0, 0)),
        compiler_params=pltpu.CompilerParams(vmem_limit_bytes=8 * MIB),
        cost_estimate=SMALL,
    )(mine, theirs)


def join_kernel(k_ref, v_ref, out_ref, sem):
    copies = [
        pltpu.make_async_copy(ref, out_ref.at[:, pl.ds(n * WIDTH, WIDTH)], sem.at[n])
        for n, ref in enumerate((k_ref, v_ref))
    ]
    for copy in copies:
        copy.start()
    for copy in copies:
        copy.wait()


def join(keys, values):
    return pl.pallas_call(
        join_kernel,
        out_shape=jax.ShapeDtypeStruct((512, 2 * WIDTH), jnp.bfloat16),
        in_specs=[pl.BlockSpec(memory_space=pl.ANY)] * 2,
        out_specs=VMEM,
        scratch_shapes=[pltpu.SemaphoreType.DMA((2,))],
        compiler_params=pltpu.CompilerParams(vmem_limit_bytes=8 * MIB),
        cost_estimate=SMALL,
    )(*(pltpu.with_memory_space_constraint(a, pltpu.HBM) for a in (keys, values)))


def project_kernel(give, *refs):
    mine, other, parts, out_ref, far = refs[:4], refs[4:8], refs[8:13], refs[13], refs[14]
    far[:128, :] = parts[2][...]
    far[128:, :] = parts[3][...]
    core_at, zl_at = lax.axis_index("core"), lax.axis_index("zl")

    def run(weights):
        def half(n, carry):
            rows = pl.ds(pl.multiple_of(n * 128, 128), 128)
            total = None
            for part, w in zip((parts[0], parts[1], far, parts[4]), weights):
                term = jnp.dot(part[rows, :], w[...], preferred_element_type=jnp.float32)
                total = term if total is None else total + term
            out_ref[rows, :] = total.astype(out_ref.dtype)
            return carry

        lax.fori_loop(0, 2, half, 0)

    same = core_at == zl_at

    @pl.when(same != give)
    def _():
        run(mine)

    @pl.when(same == give)
    def _():
        run(other)


def project(give, w_mine, w_other, parts, dtype):
    return pl.pallas_call(
        functools.partial(project_kernel, give),
        out_shape=jax.ShapeDtypeStruct((BLOCK, 640), dtype),
        in_specs=[VMEM] * 13,
        out_specs=VMEM,
        scratch_shapes=[pltpu.VMEM((BLOCK, WIDTH), jnp.bfloat16)],
        compiler_params=pltpu.CompilerParams(vmem_limit_bytes=12 * MIB),
        cost_estimate=SMALL,
    )(*w_mine, *w_other, *parts)


def together(*groups):
    flat, tree = jax.tree.flatten(groups)
    return jax.tree.unflatten(tree, lax.optimization_barrier(tuple(flat)))


def on_device(query, key_rows, value_rows, frame_seq, order, w_out):
    core_at, x_at = lax.axis_index("core"), lax.axis_index("x")

    def columns(zl, distance):
        return lax.dynamic_slice_in_dim(w_out, (zl * 4 + (x_at + distance) % 4) * 640, 640, 1)

    kv = join(key_rows, value_rows)
    kv_next = send(kv, "y", -1)
    kv_back = send(kv, "y", 1)
    q_z = send(query, "zh", 1)
    kv_core = send(kv, "core", 1)
    w_next = send(after(columns(core_at, 3), kv_core), "x", -1)
    w_back = send(after(columns(core_at, 1), kv_core), "x", 1)
    tabled = tables(order, frame_seq.reshape(64, 128))

    def attend(blocks, **named):
        return attention(blocks, tabled, (q_z, query), **named)

    near = ((0, kv), (2, kv_core))
    state = attend((2, 2), kv_parts=near)
    q_z, state = together(q_z, state)
    state_z = attend((0, 2), kv_parts=near)
    kv_next, kv_back, w_next, w_back, state, state_z = together(
        kv_next, kv_back, w_next, w_back, state, state_z
    )

    far_low = send(kv_next[:BLOCK], "y", -1)
    far_high = send(kv_back[BLOCK:], "y", 1)
    next_core = send(kv_next, "core", 1)
    back_core = send(kv_back, "core", 1)
    w_far = send(after(columns(core_at, 2), w_next), "x", 2)
    near = ((4, kv_next), (6, kv_back))
    cores = ((8, next_core), (10, back_core))
    state_z = attend((0, 2), kv_parts=near + cores, state=state_z)
    state, state_z = together(state, state_z)
    state = attend((2, 2), kv_parts=near, state=state, state_at=2)
    far_low, far_high, state_z, state = together(far_low, far_high, state_z, state)

    low_core, high_core = send(far_low, "core", 1), send(far_high, "core", 1)
    w_next_core, w_back_core = send(w_next, "core", 1), send(w_back, "core", 1)
    far = ((12, far_low), (13, far_high))
    state_z = attend((0, 2), kv_parts=far, state=state_z, tall=512)
    low_core, high_core, w_far, state_z = together(low_core, high_core, w_far, state_z)
    far_core = ((14, low_core), (15, high_core))
    w_far_core = send(w_far, "core", 1)
    got = []
    for block in range(2):
        (give,) = attend((block, 1), kv_parts=far_core, state=state_z, last=True)
        got.append(send(give, "zh", 1))
        state, give = together(state, give)
    state = attend((2, 2), kv_parts=cores, state=state, state_at=2)
    (keep,) = attend((2, 2), kv_parts=far + far_core, state=state, state_at=2, last=True, tall=512)
    keep, w_next_core, w_back_core, w_far_core = together(
        keep, w_next_core, w_back_core, w_far_core
    )
    w_mine = (columns(core_at, 0), w_next, w_far, w_back)
    w_other = (columns(1 - core_at, 0), w_next_core, w_far_core, w_back_core)

    out = []
    for block, their in enumerate(got):
        done = merge(keep, their, block)
        one, three = send(done, "x", -1), send(done, "x", 1)
        low, high = send(one[:128], "x", -1), send(three[128:], "x", 1)
        out.append([done, one, low, high, three])

    came = [
        send(project(True, w_mine, w_other, parts, jnp.bfloat16), "zl", 1) for parts in out
    ]
    kept = [project(False, w_mine, w_other, parts, jnp.float32) for parts in out]
    return jnp.concatenate(
        [(a + b.astype(jnp.float32)).astype(jnp.bfloat16) for a, b in zip(kept, came)], axis=0
    )


def solution(mesh):
    fine = Mesh(mesh.devices.reshape(4, 2, 2, 2, 4), ("y", "zh", "core", "zl", "x"))
    rows, columns = ("y", "zh", "core"), ("zl", "x")
    return jax.shard_map(
        on_device,
        mesh=fine,
        in_specs=(P(rows, columns),) * 3 + (P(), P(), P(columns, None)),
        out_specs=P(rows, columns),
        check_vma=False,
    )
```
